32 devices in a mesh: fsdp: 4 (over y, x), ctx: 8 (over z, core).
Axes of the slice: x: 2, y: 2, z: 4, core: 2. Of those that a mesh axis runs over, the one named last changes fastest.
Arguments:
- block_in: bfloat16 [4096, 1024], P(('fsdp', 'ctx')), may hold values from -6 to 6
- seq_lengths: int32 [4, 3], P('fsdp'), may hold values from 192 to 512, as said below
- norm_gain: bfloat16 [2, 1024], P(None, 'fsdp'), may hold values from 0.099609375 to 1.8984375
- in_proj: bfloat16 [2, 1024, 3352], P(None, 'fsdp'), may hold values from -0.1875 to 0.1875
- conv_weight: bfloat16 [2, 1792, 4], P(None, 'fsdp'), may hold values from -3 to 3
- conv_bias: bfloat16 [2, 1792], P(None, 'fsdp'), may hold values from -3 to 3
- dt_bias: bfloat16 [2, 24], P(None, 'fsdp'), may hold values from -3 to -1
- decay_log: bfloat16 [2, 24], P(None, 'fsdp'), may hold values from -10 to -1
- skip_gain: bfloat16 [2, 24], P(None, 'fsdp'), may hold values from 0.5 to 1.5
- mixer_gain: bfloat16 [2, 1536], P(None, 'fsdp'), may hold values from 0.099609375 to 1.8984375
- out_proj: bfloat16 [2, 1536, 1024], P(None, 'fsdp'), may hold values from -0.15625 to 0.15625
- query_proj: bfloat16 [2, 1024, 1024], P(None, 'fsdp'), may hold values from -0.1875 to 0.1875
- key_proj: bfloat16 [2, 1024, 256], P(None, 'fsdp'), may hold values from -0.1875 to 0.1875
- value_proj: bfloat16 [2, 1024, 256], P(None, 'fsdp'), may hold values from -0.1875 to 0.1875
- attn_proj: bfloat16 [2, 1024, 1024], P(None, 'fsdp'), may hold values from -1.5 to 1.5
- ffn_gain: bfloat16 [2, 1024], P(None, 'fsdp'), may hold values from 0.099609375 to 1.8984375
- gate_proj: bfloat16 [2, 1024, 2048], P(None, 'fsdp'), may hold values from -0.1875 to 0.1875
- up_proj: bfloat16 [2, 1024, 2048], P(None, 'fsdp'), may hold values from -0.1875 to 0.1875
- down_proj: bfloat16 [2, 2048, 1024], P(None, 'fsdp'), may hold values from -0.125 to 0.125
- out_grad: bfloat16 [4096, 1024], P(('fsdp', 'ctx')), may hold values from -6 to 6
Outputs:
- block_out: bfloat16 [4096, 1024], P(('fsdp', 'ctx'))
- in_grad: bfloat16 [4096, 1024], P(('fsdp', 'ctx'))
- grad_norm_gain: float32 [2, 1024], P(None, 'fsdp')
- grad_in_proj: float32 [2, 1024, 3352], P(None, 'fsdp')
- grad_conv_weight: float32 [2, 1792, 4], P(None, 'fsdp')
- grad_conv_bias: float32 [2, 1792], P(None, 'fsdp')
- grad_dt_bias: float32 [2, 24], P(None, 'fsdp')
- grad_decay_log: float32 [2, 24], P(None, 'fsdp')
- grad_skip_gain: float32 [2, 24], P(None, 'fsdp')
- grad_mixer_gain: float32 [2, 1536], P(None, 'fsdp')
- grad_out_proj: float32 [2, 1536, 1024], P(None, 'fsdp')
- grad_query_proj: float32 [2, 1024, 1024], P(None, 'fsdp')
- grad_key_proj: float32 [2, 1024, 256], P(None, 'fsdp')
- grad_value_proj: float32 [2, 1024, 256], P(None, 'fsdp')
- grad_attn_proj: float32 [2, 1024, 1024], P(None, 'fsdp')
- grad_ffn_gain: float32 [2, 1024], P(None, 'fsdp')
- grad_gate_proj: float32 [2, 1024, 2048], P(None, 'fsdp')
- grad_up_proj: float32 [2, 1024, 2048], P(None, 'fsdp')
- grad_down_proj: float32 [2, 2048, 1024], P(None, 'fsdp')
The draws below stay inside these ranges and needn't reach their ends.
Inputs may be any that keep to these rules, and one draw needn't show every extreme that they name: `seq_lengths`: row f lists the lengths of the 3 sequences of fsdp index f in the order in which their pieces lie on every ctx device; each length is a multiple of the number of ctx devices, a row sums to 1024, and the longest of every row is exactly half of that.
All inputs are finite; a program needn't handle non-finite values.
Results may differ from the reference program's by a relative error of at most 0.039.
Values may be sent and summed in bfloat16 or wider, within the bound.
No kernel may reach another device: no remote copies, remote signals or barrier semaphores. Data moves between devices by JAX's collectives and lax.ppermute only.
A program may use at most 448 MiB of HBM per device.

```python
import math
import jax
import jax.numpy as jnp
from jax import lax

D = 1024
QH = 8
KVH = 2
HD = 128
MH = 24
MP = 64
NS = 128
FF = 2048
CONV = 4
LAYERS = 2
SEQS = 3
TOK_DEV = 128
DSSM = 1536
CONVCH = 1792
PROJ = 3352
TOKENS = 4096
N_FSDP = 4
N_CTX = 8


def draw_seq_lengths(key, part):
    key = jax.random.fold_in(key, 7)
    half_rows = TOK_DEV // 2
    least_rows = TOK_DEV * 3 // 16
    spare_rows = half_rows - (SEQS - 1) * least_rows

    def one_row(row_key):
        cut_key, order_key = jax.random.split(row_key)
        cut_points = jnp.sort(jax.random.randint(cut_key, (SEQS - 2,), 0, spare_rows + 1, dtype=jnp.int32))
        bounds = jnp.concatenate([jnp.zeros((1,), jnp.int32), cut_points, jnp.full((1,), spare_rows, jnp.int32)])
        part_sizes = bounds[1:] - bounds[:-1] + least_rows
        values = jnp.concatenate([jnp.full((1,), half_rows, jnp.int32), part_sizes])
        ordering = jax.random.permutation(order_key, SEQS)
        return values[ordering] * N_CTX
    return jax.vmap(one_row)(jax.random.split(key, N_FSDP)).astype(jnp.int32)


def level_of(key, extent, shards, least, high):
    level, own = 1.0, jax.random.fold_in(key, 6)
    for dim, parts in shards:
        steps = jnp.exp(jax.random.uniform(jax.random.fold_in(own, dim), (parts,), jnp.float32, least / len(shards), high / len(shards)))
        level = level * jnp.repeat(steps, extent[dim] // parts).reshape([-1 if axis == dim else 1 for axis in range(len(extent))])
    return level


def gaussian(stream_key, shape, spread, limit, cuts=(), kind=jnp.bfloat16):
    drawn = spread * jax.random.normal(stream_key, shape, jnp.float32)
    if cuts:
        drawn = drawn * level_of(stream_key, shape, cuts, -0.22, 0.18)
    return jnp.clip(drawn, -limit, limit).astype(kind)


def setup_inputs(seed: int = 0) -> dict:
    keys = jax.random.split(jax.random.key(seed), 21)
    block_in = gaussian(keys[0], (TOKENS, D), 1.0, 6.0, ((0, 32),))
    seq_lengths = draw_seq_lengths(jax.random.fold_in(keys[20], 71), 0)
    norm_gain = jnp.clip(1.0 + 0.18 * jax.random.normal(keys[2], (LAYERS, D), jnp.float32), 0.099609375, 1.8984375).astype(jnp.bfloat16)
    in_proj = gaussian(keys[3], (LAYERS, D, PROJ), D ** -0.5, 0.1875, ((1, 4),))
    conv_weight = gaussian(keys[4], (LAYERS, CONVCH, CONV), CONV ** -0.5, 3.0, ((1, 4),))
    conv_bias = gaussian(keys[5], (LAYERS, CONVCH), 0.5, 3.0, ((1, 4),))
    dt_bias = jnp.clip(-3.0 + 2.0 * jax.random.uniform(keys[6], (LAYERS, MH), jnp.float32) ** level_of(keys[6], (LAYERS, MH), ((1, 4),), -0.2, 0.2), -3.0, -1.0).astype(jnp.bfloat16)
    decay_log = jnp.clip(-10.0 + 9.0 * jax.random.uniform(keys[7], (LAYERS, MH), jnp.float32) ** level_of(keys[7], (LAYERS, MH), ((1, 4),), -0.2, 0.2), -10.0, -1.0).astype(jnp.bfloat16)
    skip_gain = jnp.clip(0.5 + 1.0 * jax.random.uniform(keys[8], (LAYERS, MH), jnp.float32) ** level_of(keys[8], (LAYERS, MH), ((1, 4),), -0.2, 0.2), 0.5, 1.5).astype(jnp.bfloat16)
    mixer_gain = jnp.clip(1.0 + 0.18 * jax.random.normal(keys[9], (LAYERS, DSSM), jnp.float32), 0.099609375, 1.8984375).astype(jnp.bfloat16)
    out_proj = gaussian(keys[10], (LAYERS, DSSM, D), DSSM ** -0.5, 0.15625, ((1, 4),))
    query_proj = gaussian(keys[11], (LAYERS, D, QH * HD), D ** -0.5, 0.1875, ((1, 4),))
    key_proj = gaussian(keys[12], (LAYERS, D, KVH * HD), D ** -0.5, 0.1875, ((1, 4),))
    value_proj = gaussian(keys[13], (LAYERS, D, KVH * HD), D ** -0.5, 0.1875, ((1, 4),))
    attn_proj = gaussian(keys[14], (LAYERS, QH * HD, D), (QH * HD // 64) ** -0.5, 1.5, ((1, 4),))
    ffn_gain = jnp.clip(1.0 + 0.18 * jax.random.normal(keys[15], (LAYERS, D), jnp.float32), 0.099609375, 1.8984375).astype(jnp.bfloat16)
    gate_proj = gaussian(keys[16], (LAYERS, D, FF), D ** -0.5, 0.1875, ((1, 4),))
    up_proj = gaussian(keys[17], (LAYERS, D, FF), D ** -0.5, 0.1875, ((1, 4),))
    down_proj = gaussian(keys[18], (LAYERS, FF, D), FF ** -0.5, 0.125, ((1, 4),))
    out_grad = gaussian(keys[19], (TOKENS, D), 1.0, 6.0, ((0, 32),))
    return dict(block_in=block_in, seq_lengths=seq_lengths, norm_gain=norm_gain, in_proj=in_proj, conv_weight=conv_weight, conv_bias=conv_bias, dt_bias=dt_bias, decay_log=decay_log, skip_gain=skip_gain, mixer_gain=mixer_gain, out_proj=out_proj, query_proj=query_proj, key_proj=key_proj, value_proj=value_proj, attn_proj=attn_proj, ffn_gain=ffn_gain, gate_proj=gate_proj, up_proj=up_proj, down_proj=down_proj, out_grad=out_grad)


EPSILON = 1e-05
ROPE_BASE = 100000000000.0
MASKED = -1e+30
HIGHEST = lax.Precision.HIGHEST

@jax.custom_vjp
def low(v):
    return lax.optimization_barrier(v.astype(jnp.bfloat16)).astype(jnp.float32)

@jax.custom_vjp
def low_back(v):
    return v

def low_keep(v):
    return (low(v), None)

def low_pass(kept, grad):
    return (grad,)

def back_keep(v):
    return (v, None)

def back_low(kept, grad):
    return (low(grad),)
low.defvjp(low_keep, low_pass)
low_back.defvjp(back_keep, back_low)

def product(matrix_a, matrix_b):
    return jnp.dot(matrix_a, matrix_b, precision=HIGHEST, preferred_element_type=jnp.float32)

def rms_scale(values, gain_vec):
    return values * lax.rsqrt(lax.optimization_barrier(jnp.mean(values * values, axis=-1, keepdims=True)) + EPSILON) * gain_vec

def layout(pieces, device, local_rows):
    piece_ends = jnp.cumsum(pieces).astype(jnp.int32)
    piece_starts = (piece_ends - pieces).astype(jnp.int32)
    member = (local_rows[:, None] >= piece_starts[None, :]) & (local_rows[:, None] < piece_ends[None, :])
    numbers = jnp.arange(SEQS, dtype=jnp.int32)
    sequence = lax.optimization_barrier(jnp.sum(jnp.where(member, numbers[None, :], 0), axis=1)).astype(jnp.int32)
    begin_row = lax.optimization_barrier(jnp.sum(jnp.where(member, piece_starts[None, :], 0), axis=1)).astype(jnp.int32)
    piece_len = lax.optimization_barrier(jnp.sum(jnp.where(member, pieces[None, :], 0), axis=1)).astype(jnp.int32)
    position = (device * piece_len + local_rows - begin_row).astype(jnp.int32)
    return (member, sequence, position, begin_row, piece_ends)

def rotate(vectors, position):
    half_dim = vectors.shape[-1] // 2
    frequency = jnp.exp(-math.log(ROPE_BASE) * jnp.arange(half_dim, dtype=jnp.float32) / half_dim)
    angles = position.astype(jnp.float32)[:, None] * frequency[None, :]
    cosine = jnp.cos(angles)[:, None, :]
    sine_val = jnp.sin(angles)[:, None, :]
    first_half = vectors[..., :half_dim]
    second_half = vectors[..., half_dim:]
    return jnp.concatenate([first_half * cosine - second_half * sine_val, second_half * cosine + first_half * sine_val], axis=-1)

def project_in(hidden, norm_gain, in_proj, query_proj, key_proj, value_proj, position):
    row_count = hidden.shape[0]
    normed = low(rms_scale(hidden, norm_gain))
    projected = low_back(low(product(normed, in_proj)))
    queries = low_back(low(rotate(product(normed, query_proj).reshape(row_count, QH, HD), position).reshape(row_count, QH * HD)))
    keys_out = low_back(low(rotate(product(normed, key_proj).reshape(row_count, KVH, HD), position).reshape(row_count, KVH * HD)))
    values_out = low_back(low(product(normed, value_proj)))
    return (projected, queries, keys_out, values_out)

def take_tails(projected, piece_ends):
    offsets = jnp.arange(CONV - 1, dtype=jnp.int32)
    tail_rows = piece_ends[:, None] - (CONV - 1) + offsets[None, :]
    return projected[:, DSSM:DSSM + CONVCH][tail_rows]

def scan_block(projected, previous, conv_weight, conv_bias, dt_bias, decay_log, skip_gain, member, sequence, begin_row, piece_ends):
    row_count = projected.shape[0]
    row_ids = jnp.arange(row_count, dtype=jnp.int32)
    conv_in = projected[:, DSSM:DSSM + CONVCH]
    conv_sum = conv_bias[None, :] + conv_weight[:, CONV - 1][None, :] * conv_in
    for lag_rows in range(1, CONV):
        shifted = jnp.concatenate([jnp.zeros((lag_rows, CONVCH), conv_in.dtype), conv_in[:row_count - lag_rows]], axis=0)
        before = begin_row - (row_ids - lag_rows)
        fetched = previous[sequence, jnp.clip(CONV - 1 - before, 0, CONV - 2)]
        conv_sum = conv_sum + conv_weight[:, CONV - 1 - lag_rows][None, :] * jnp.where((before > 0)[:, None], fetched, shifted)
    conv_out = low(jax.nn.silu(conv_sum))
    inputs = conv_out[:, :DSSM].reshape(row_count, MH, MP)
    b_mat = conv_out[:, DSSM:DSSM + NS]
    c_mat = conv_out[:, DSSM + NS:]
    step_dt = jax.nn.softplus(projected[:, DSSM + CONVCH:] + dt_bias[None, :])
    log_decay = -step_dt * jnp.exp(decay_log)[None, :]
    running = jnp.cumsum(log_decay, axis=0)
    seg_cum = running - (running - log_decay)[begin_row]
    causal = (sequence[:, None] == sequence[None, :]) & (row_ids[:, None] >= row_ids[None, :])
    gap_log = jnp.where(causal[None], running.T[:, :, None] - running.T[:, None, :], MASKED)
    kernel = jnp.exp(gap_log) * jnp.dot(c_mat, b_mat.T, precision=HIGHEST)[None] * step_dt.T[:, None, :]
    y_part = jnp.einsum('hij,jhp->ihp', kernel, inputs, precision=HIGHEST) + skip_gain[None, :, None] * inputs
    seg_end = seg_cum[piece_ends - 1]
    decay_total = jnp.exp(seg_end)
    weight_end = jnp.exp(seg_end[sequence] - seg_cum) * step_dt
    member_f = member.astype(jnp.float32)
    end_state = jnp.einsum('js,jh,jhp,jn->shpn', member_f, weight_end, inputs, b_mat, precision=HIGHEST)
    return (y_part, c_mat, seg_cum, decay_total, end_state)

def mixer_out(y_part, c_mat, seg_cum, state_in, projected, mixer_gain, out_proj, member):
    row_count = y_part.shape[0]
    member_f = member.astype(jnp.float32)
    carried = jnp.einsum('in,shpn->sihp', c_mat, state_in, precision=HIGHEST)
    carried = jnp.einsum('is,sihp->ihp', member_f, carried, precision=HIGHEST) * jnp.exp(seg_cum)[:, :, None]
    gated = (y_part + carried).reshape(row_count, DSSM) * jax.nn.silu(projected[:, :DSSM])
    return low_back(product(low(rms_scale(gated, mixer_gain)), out_proj))

def piece_back(hidden, mamba_out, attended, attn_proj, ffn_gain, gate_proj, up_proj, down_proj):
    mid_sum = hidden + mamba_out + low_back(product(attended, attn_proj))
    normed = low(rms_scale(mid_sum, ffn_gain))
    gate_val = low_back(product(normed, gate_proj))
    up_val = low_back(product(normed, up_proj))
    act_val = low(jax.nn.silu(gate_val) * up_val)
    return mid_sum + low_back(product(act_val, down_proj))

def layer_group(hidden, pieces, weights):
    norm_gain, in_proj, conv_weight, conv_bias, dt_bias, decay_log, skip_gain, mixer_gain, out_proj, query_proj, key_proj, value_proj, attn_proj, ffn_gain, gate_proj, up_proj, down_proj = weights
    total_rows = hidden.shape[0]
    row_ids = jnp.arange(total_rows, dtype=jnp.int32)
    _, sequence, position, _, piece_ends = layout(pieces, row_ids // TOK_DEV, row_ids % TOK_DEV)
    projected, queries, keys_all, values_all = project_in(hidden, norm_gain, in_proj, query_proj, key_proj, value_proj, position)
    local_ids = jnp.arange(TOK_DEV, dtype=jnp.int32)
    block_member, block_seq, _, block_begin, _ = layout(pieces, 0, local_ids)

    def device_step(carry_in, projected_block):
        state, tails_prev = carry_in
        y_part, c_mat, seg_cum, decay_total, end_state = scan_block(projected_block, tails_prev, conv_weight, conv_bias, dt_bias, decay_log, skip_gain, block_member, block_seq, block_begin, piece_ends)
        mixed_out = mixer_out(y_part, c_mat, seg_cum, state, projected_block, mixer_gain, out_proj, block_member)
        state = decay_total[:, :, None, None] * state + end_state
        return ((state, take_tails(projected_block, piece_ends)), mixed_out)
    start_carry = (jnp.zeros((SEQS, MH, MP, NS), jnp.float32), jnp.zeros((SEQS, CONV - 1, CONVCH), jnp.float32))
    _, mamba_out = lax.scan(jax.checkpoint(device_step), start_carry, projected.reshape(total_rows // TOK_DEV, TOK_DEV, PROJ))
    mamba_out = mamba_out.reshape(total_rows, D)
    query_block = min(512, total_rows)
    group_size = QH // KVH
    key_heads = keys_all.reshape(total_rows, KVH, HD)
    value_heads = values_all.reshape(total_rows, KVH, HD)

    def attend(block_args):
        q_blk, seq_blk, pos_blk = block_args
        q_heads = q_blk.reshape(query_block, KVH, group_size, HD)
        raw_scores = jnp.einsum('qkgd,nkd->kgqn', q_heads, key_heads, precision=HIGHEST)
        scores = low_back(raw_scores * HD ** (-0.5))
        allowed = (seq_blk[:, None] == sequence[None, :]) & (position[None, :] <= pos_blk[:, None])
        masked = jnp.where(allowed[None, None], scores, MASKED)
        log_total = jax.nn.logsumexp(masked, axis=-1, keepdims=True)
        prob_blk = jnp.exp(masked - log_total)
        result = jnp.einsum('kgqn,nkd->qkgd', prob_blk, value_heads, precision=HIGHEST)
        return low_back(low(result.reshape(query_block, QH * HD)))
    attended = lax.map(jax.checkpoint(attend), (queries.reshape(total_rows // query_block, query_block, QH * HD), sequence.reshape(total_rows // query_block, query_block), position.reshape(total_rows // query_block, query_block)))
    attended = attended.reshape(total_rows, QH * HD)
    return piece_back(hidden, mamba_out, attended, attn_proj, ffn_gain, gate_proj, up_proj, down_proj)

def forward(block_in, seq_lengths, weights):
    groups = block_in.reshape(N_FSDP, N_CTX * TOK_DEV, D)
    results = []
    for group_idx in range(N_FSDP):
        hidden = groups[group_idx]
        pieces = (seq_lengths[group_idx] // N_CTX).astype(jnp.int32)
        for layer_idx in range(LAYERS):
            hidden = layer_group(hidden, pieces, tuple((weight_arr[layer_idx] for weight_arr in weights)))
        results.append(hidden)
    return jnp.concatenate(results, axis=0)

def reference(block_in, seq_lengths, norm_gain, in_proj, conv_weight, conv_bias, dt_bias, decay_log, skip_gain, mixer_gain, out_proj, query_proj, key_proj, value_proj, attn_proj, ffn_gain, gate_proj, up_proj, down_proj, out_grad):
    weights32 = tuple((weight_arr.astype(jnp.float32) for weight_arr in (norm_gain, in_proj, conv_weight, conv_bias, dt_bias, decay_log, skip_gain, mixer_gain, out_proj, query_proj, key_proj, value_proj, attn_proj, ffn_gain, gate_proj, up_proj, down_proj)))

    def run_all(hidden, *params):
        return forward(hidden, seq_lengths, params)
    result, pullback = jax.vjp(run_all, block_in.astype(jnp.float32), *weights32)
    grads = pullback(out_grad.astype(jnp.float32))
    return (result.astype(jnp.bfloat16), grads[0].astype(jnp.bfloat16), grads[1], grads[2], grads[3], grads[4], grads[5], grads[6], grads[7], grads[8], grads[9], grads[10], grads[11], grads[12], grads[13], grads[14], grads[15], grads[16], grads[17])
```

```python
import math

import jax
import jax.numpy as jnp
from jax import lax
from jax.sharding import Mesh, PartitionSpec as P

QH = 8
KVH = 2
HD = 128
MH = 24
MP = 64
NS = 128
CONV = 4
LAYERS = 2
SEQS = 3
DSSM = 1536
CONVCH = 1792
TP = 8
ZZ = 4
PAR = 2
HEADS = MH // TP
XW = HEADS * MP
CW = XW + 2 * NS
CHUNK = 128

EPSILON = 1e-05
ROPE_BASE = 100000000000.0
MASKED = -1e30
BF = jnp.bfloat16
F32 = jnp.float32
TPA = ("zz", "par")


def dot(a, b):
    return jnp.dot(a, b, preferred_element_type=F32)


def dot_nt(a, b):
    return lax.dot_general(a, b, (((1,), (1,)), ((), ())), preferred_element_type=F32)


def dot_tn(a, b):
    return lax.dot_general(a, b, (((0,), (0,)), ((), ())), preferred_element_type=F32)


def rotate(vectors, cosine, sine):
    half = HD // 2
    a = vectors[:, :half]
    b = vectors[:, half:]
    return jnp.concatenate([a * cosine - b * sine, b * cosine + a * sine], axis=-1)


def one_hot(index, count):
    return (index[:, None] == jnp.arange(count, dtype=jnp.int32)[None, :]).astype(BF)


def inv_rms(values):
    return lax.rsqrt(jnp.mean(values * values, axis=-1, keepdims=True) + EPSILON)


def rms_back(grad_y, values, inv, gain):
    scaled = values * inv
    gg = grad_y * gain
    grad_v = (gg - scaled * jnp.mean(gg * scaled, axis=-1, keepdims=True)) * inv
    grad_g = jnp.sum(grad_y * scaled, axis=0)
    return grad_v, grad_g


def ssd_local(conv_in, dt_raw, conv_weight, conv_bias, dt_bias, decay_log, skip_gain, seg, pos):
    rows = conv_in.shape[0]
    conv_sum = conv_bias[None, :] + conv_weight[CONV - 1][None, :] * conv_in
    for lag in range(1, CONV):
        shifted = jnp.concatenate(
            [jnp.zeros((lag, CW), conv_in.dtype), conv_in[: rows - lag]], axis=0
        )
        conv_sum = conv_sum + conv_weight[CONV - 1 - lag][None, :] * jnp.where(
            (pos >= lag)[:, None], shifted, 0.0
        )
    conv_out = jax.nn.silu(conv_sum)
    rounded = lax.optimization_barrier(conv_out.astype(BF)).astype(F32)
    conv_out = conv_out + lax.stop_gradient(rounded - conv_out)
    chunks = rows // CHUNK
    xs = conv_out[:, :XW].reshape(chunks, CHUNK, HEADS, MP)
    bm = conv_out[:, XW : XW + NS].reshape(chunks, CHUNK, NS)
    cm = conv_out[:, XW + NS :].reshape(chunks, CHUNK, NS)
    dt = jax.nn.softplus(dt_raw + dt_bias[None, :]).reshape(chunks, CHUNK, HEADS)
    la = -dt * jnp.exp(decay_log)
    cum = jnp.cumsum(la, axis=1)
    sg = seg.reshape(chunks, CHUNK)
    causal = (sg[:, :, None] == sg[:, None, :]) & jnp.tril(jnp.ones((CHUNK, CHUNK), bool))[None]
    cum_t = cum.transpose(0, 2, 1)
    dt_t = dt.transpose(0, 2, 1)
    gap = jnp.where(causal[:, None], cum_t[:, :, :, None] - cum_t[:, :, None, :], MASKED)
    cb = jnp.einsum("cin,cjn->cij", cm, bm)
    kern = jnp.exp(gap) * cb[:, None] * dt_t[:, :, None, :]
    y = jnp.einsum("chij,cjhp->cihp", kern, xs)
    last = cum[:, -1, :]
    wend = (
        jnp.exp(last[:, None, :] - cum) * dt * (sg == sg[:, -1:]).astype(F32)[:, :, None]
    )
    ends = jnp.einsum("cjh,cjhp,cjn->chpn", wend, xs, bm)
    running = jnp.cumsum(last, axis=0)
    before = running - last
    ids = jnp.arange(chunks)
    seg_last = sg[:, -1]
    prev_seg = jnp.concatenate([jnp.full((1,), -1, seg_last.dtype), seg_last[:-1]])
    flows = (ids[:, None] > ids[None, :]) & (prev_seg[:, None] == seg_last[None, :])
    carry = jnp.exp(jnp.where(flows[:, :, None], before[:, None, :] - running[None, :, :], MASKED))
    state_in = jnp.einsum("cdh,dhpn->chpn", carry, ends)
    win = jnp.exp(cum) * (sg == prev_seg[:, None]).astype(F32)[:, :, None]
    y = y + jnp.einsum("cin,chpn->cihp", cm, state_in) * win[..., None]
    y = y + skip_gain[None, None, :, None] * xs
    return y.reshape(rows, XW)


def attn_block(q, k, seg_q, pos_q, seg, pos):
    scores = dot_nt(q, k) * HD ** (-0.5)
    allowed = (seg_q[:, None] == seg[None, :]) & (pos[None, :] <= pos_q[:, None])
    return jnp.where(allowed, scores, MASKED)


def in_blocks(step, carry, arrays):
    rows = arrays[0].shape[0]
    size = min(rows, 1024 * 1024 // rows)
    if size == rows:
        return step(carry, arrays)
    split = tuple(a.reshape((rows // size, size) + a.shape[1:]) for a in arrays)
    carry, outs = lax.scan(step, carry, split)
    return carry, jax.tree.map(lambda o: o.reshape((rows,) + o.shape[2:]), outs)


def attn_forward(q, k, v, seg, pos):
    def step(carry, block):
        q_b, seg_b, pos_b = block
        scores = attn_block(q_b, k, seg_b, pos_b, seg, pos)
        top = jnp.max(scores, axis=-1, keepdims=True)
        prob = jnp.exp(scores - top)
        total = jnp.sum(prob, axis=-1, keepdims=True)
        return carry, (dot(prob.astype(BF), v) / total, top + jnp.log(total))

    return in_blocks(step, 0.0, (q, seg, pos))[1]


def attn_backward(q, k, v, grad, delta, logs, seg, pos):
    def step(carry, block):
        q_b, grad_b, delta_b, logs_b, seg_b, pos_b = block
        prob = jnp.exp(attn_block(q_b, k, seg_b, pos_b, seg, pos) - logs_b)
        gs = (prob * (dot_nt(grad_b, v) - delta_b)).astype(BF)
        gk = carry[0] + dot_tn(gs, q_b) * HD ** (-0.5)
        gv = carry[1] + dot_tn(prob.astype(BF), grad_b)
        return (gk, gv), dot(gs, k) * HD ** (-0.5)

    zero = jnp.zeros(k.shape, F32)
    (gk, gv), gq = in_blocks(step, (zero, zero), (q, grad, delta, logs, seg, pos))
    return gq, gk, gv


def layer_forward(h, w, meta):
    seg, pos, cosine, sine = meta
    inv1 = inv_rms(h)
    normed = (h * inv1 * w["norm_gain"]).astype(BF)
    pr = dot(normed, w["w1"])
    proj = pr[:, :768].astype(BF)
    q = rotate(pr[:, 768:896], cosine, sine).astype(BF)
    k = rotate(pr[:, 896:1024], cosine, sine).astype(BF)
    v = pr[:, 1024:1152].astype(BF)
    z = proj[:, :XW].astype(F32)
    conv_in = proj[:, XW : XW + CW].astype(F32)
    dt_raw = proj[:, XW + CW : XW + CW + HEADS].astype(F32)

    def run(ci, dr, cw, cb, db, dl, sk):
        return ssd_local(ci, dr, cw, cb, db, dl, sk, seg, pos)

    ssd, pull = jax.vjp(
        run,
        conv_in,
        dt_raw,
        w["conv_weight"],
        w["conv_bias"],
        w["dt_bias"],
        w["decay_log"],
        w["skip_gain"],
    )
    gated = ssd * jax.nn.silu(z)
    square = lax.psum(jnp.sum(gated * gated, axis=-1), TPA)
    attended, logs = attn_forward(q, k, v, seg, pos)
    inv_g = lax.rsqrt(square / DSSM + EPSILON)[:, None]
    mixer = (gated * inv_g * w["mixer_gain"]).astype(BF)
    att_low = attended.astype(BF)
    mixed = jnp.concatenate([mixer, att_low], axis=1)
    mid = h + lax.psum(dot(mixed, w["wr"][: XW + HD]).astype(BF), TPA).astype(F32)
    inv2 = inv_rms(mid)
    normed2 = (mid * inv2 * w["ffn_gain"]).astype(BF)
    gu = dot(normed2, w["w2"])
    ff = gu.shape[1] // 2
    act = (jax.nn.silu(gu[:, :ff]) * gu[:, ff:]).astype(BF)
    kept = dict(
        h=h, inv1=inv1, normed=normed, z=z, ssd=ssd, gated=gated, pull=pull, inv_g=inv_g,
        q=q, k=k, v=v, attended=attended, logs=logs, mixed=mixed, mid=mid, inv2=inv2,
        normed2=normed2, gu=gu, act=act,
    )
    return mid, act, kept


def layer_backward(gout, w, kept, meta):
    seg, pos, cosine, sine = meta
    g_down = gout.astype(BF)
    g_act = dot_nt(g_down, w["wr"][XW + HD :])
    d_down = dot_tn(kept["act"], g_down)
    ff = kept["gu"].shape[1] // 2
    gate, up = kept["gu"][:, :ff], kept["gu"][:, ff:]
    sig = jax.nn.sigmoid(gate)
    g_gate = g_act * up * sig * (1.0 + gate * (1.0 - sig))
    g_up = g_act * gate * sig
    g_gu = jnp.concatenate([g_gate.astype(BF), g_up.astype(BF)], axis=1)
    g_n2 = lax.psum(dot_nt(g_gu, w["w2"]).astype(BF), TPA).astype(F32)
    d_w2 = dot_tn(kept["normed2"], g_gu)
    g_mid, d_ffn_gain = rms_back(g_n2, kept["mid"], kept["inv2"], w["ffn_gain"])
    g_mid = gout + g_mid
    g_low = g_mid.astype(BF)
    g_mixed = dot_nt(g_low, w["wr"][: XW + HD])
    d_wr = dot_tn(kept["mixed"], g_low)
    g_mix = g_mixed[:, :XW]
    scaled = kept["gated"] * kept["inv_g"]
    gg = g_mix * w["mixer_gain"]
    d_mixer_gain = jnp.sum(g_mix * scaled, axis=0)
    mean = lax.psum(jnp.sum(gg * scaled, axis=-1), TPA)[:, None] / DSSM
    g_att = g_mixed[:, XW:].astype(BF)
    delta = jnp.sum(g_att.astype(F32) * kept["attended"], axis=-1, keepdims=True)
    gq, gk, gv = attn_backward(
        kept["q"], kept["k"], kept["v"], g_att, delta, kept["logs"], seg, pos
    )
    gq = rotate(gq.astype(BF).astype(F32), cosine, -sine).astype(BF)
    gk = rotate(gk.astype(BF).astype(F32), cosine, -sine).astype(BF)
    g_gated = (gg - scaled * mean) * kept["inv_g"]
    z = kept["z"]
    sz = jax.nn.sigmoid(z)
    g_ssd = g_gated * z * sz
    g_z = g_gated * kept["ssd"] * sz * (1.0 + z * (1.0 - sz))
    g_conv, g_dt, d_cw, d_cb, d_db, d_dl, d_sk = kept["pull"](g_ssd)
    rows = gout.shape[0]
    g_pr = jnp.concatenate(
        [
            g_z.astype(BF),
            g_conv.astype(BF),
            g_dt.astype(BF),
            jnp.zeros((rows, 128 - HEADS), BF),
            gq,
            gk,
            gv.astype(BF),
        ],
        axis=1,
    )
    g_n1 = lax.psum(dot_nt(g_pr, w["w1"]).astype(BF), TPA).astype(F32)
    d_w1 = dot_tn(kept["normed"], g_pr)
    g_h, d_norm_gain = rms_back(g_n1, kept["h"], kept["inv1"], w["norm_gain"])
    small = (d_norm_gain, d_cw, d_cb, d_db, d_dl, d_sk, d_mixer_gain, d_ffn_gain)
    return g_mid + g_h, (d_w1, d_w2, d_wr, d_down), small


def per_device(
    block_in,
    seq_lengths,
    norm_gain,
    in_proj,
    conv_weight,
    conv_bias,
    dt_bias,
    decay_log,
    skip_gain,
    mixer_gain,
    out_proj,
    query_proj,
    key_proj,
    value_proj,
    attn_proj,
    ffn_gain,
    gate_proj,
    up_proj,
    down_proj,
    out_grad,
):
    fs = lax.axis_size("fsdp")
    reps = lax.axis_size("rep")
    ctx = reps * TP
    own_rows, width = block_in.shape
    rows = ctx * own_rows
    f = lax.axis_index("fsdp")
    rep = lax.axis_index("rep")
    t = lax.axis_index(TPA)
    every = ("rep",) + TPA

    lengths = seq_lengths[0]
    ends = jnp.cumsum(lengths)
    starts = ends - lengths
    line = jnp.arange(rows, dtype=jnp.int32)
    seg = jnp.sum((line[:, None] >= ends[None, :]).astype(jnp.int32), axis=1)
    pos = line - jnp.sum(jnp.where(seg[:, None] == jnp.arange(SEQS)[None, :], starts[None, :], 0), axis=1)
    pieces = lengths // ctx
    p_ends = jnp.cumsum(pieces)
    p_starts = p_ends - pieces
    local = line % own_rows
    piece = line // own_rows
    l_seg = jnp.sum((local[:, None] >= p_ends[None, :]).astype(jnp.int32), axis=1)
    pick = l_seg[:, None] == jnp.arange(SEQS)[None, :]
    place = (
        jnp.sum(jnp.where(pick, starts[None, :] - p_starts[None, :] + piece[:, None] * pieces[None, :], 0), axis=1)
        + local
    )
    half = HD // 2
    frequency = jnp.exp(-math.log(ROPE_BASE) * jnp.arange(half, dtype=F32) / half)
    angles = pos.astype(F32)[:, None] * frequency[None, :]
    meta = (seg, pos, jnp.cos(angles), jnp.sin(angles))

    to_seq = one_hot(place, rows).T
    x_all = lax.all_gather(block_in, every, axis=0, tiled=True)

    def columns(layer):
        pieces_1 = [
            lax.dynamic_slice_in_dim(in_proj[layer], XW * t, XW, 1),
            lax.dynamic_slice_in_dim(in_proj[layer], DSSM + XW * t, XW, 1),
            in_proj[layer][:, 2 * DSSM : DSSM + CONVCH],
            lax.dynamic_slice_in_dim(in_proj[layer], DSSM + CONVCH + HEADS * t, HEADS, 1),
            jnp.zeros((in_proj.shape[1], 128 - HEADS), BF),
            lax.dynamic_slice_in_dim(query_proj[layer], HD * t, HD, 1),
            lax.dynamic_slice_in_dim(key_proj[layer], HD * (t * KVH // TP), HD, 1),
            lax.dynamic_slice_in_dim(value_proj[layer], HD * (t * KVH // TP), HD, 1),
        ]
        ff = gate_proj.shape[2] // TP
        pieces_2 = [
            lax.dynamic_slice_in_dim(gate_proj[layer], ff * t, ff, 1),
            lax.dynamic_slice_in_dim(up_proj[layer], ff * t, ff, 1),
        ]
        return jnp.concatenate(pieces_1, 1), jnp.concatenate(pieces_2, 1)

    par = t % PAR
    ff = gate_proj.shape[2] // TP

    def row_pieces(layer):
        return jnp.concatenate(
            [
                lax.dynamic_slice_in_dim(out_proj[layer], XW * par, XW, 0),
                lax.dynamic_slice_in_dim(attn_proj[layer], HD * par, HD, 0),
                lax.dynamic_slice_in_dim(down_proj[layer], ff * par, ff, 0),
            ],
            0,
        )

    forth = []
    for s in range(fs):
        for r in range(reps):
            for c in range(TP):
                src = (s * reps + r) * TP + c
                dst = ((c // PAR) * reps + r) * TP + PAR * s + c % PAR
                forth.append((src, dst))
    back = [(b, a) for a, b in forth]
    axes = ("fsdp",) + every

    smalls = jnp.concatenate(
        [
            norm_gain,
            conv_weight.transpose(0, 2, 1).reshape(LAYERS, -1),
            conv_bias,
            dt_bias,
            decay_log,
            skip_gain,
            mixer_gain,
            ffn_gain,
        ],
        axis=1,
    )
    small_all = lax.all_gather(smalls, "fsdp", axis=0)
    w1_own, w2_own = zip(*[columns(layer) for layer in range(LAYERS)])
    w1 = [None, None]
    w2 = [None, None]
    wr = [None, None]
    for layer in range(LAYERS):
        w1[layer] = lax.all_gather(w1_own[layer], "fsdp", axis=0, tiled=True)
        wr[layer] = lax.ppermute(row_pieces(layer), axes, forth)
        w2[layer] = lax.all_gather(w2_own[layer], "fsdp", axis=0, tiled=True)
    g_all = lax.all_gather(out_grad, every, axis=0, tiled=True)

    sizes = [
        norm_gain.shape[1],
        CONV * conv_weight.shape[1],
        conv_bias.shape[1],
        dt_bias.shape[1],
        decay_log.shape[1],
        skip_gain.shape[1],
        mixer_gain.shape[1],
        ffn_gain.shape[1],
    ]
    offsets = [sum(sizes[:i]) for i in range(len(sizes) + 1)]

    def own_conv(full):
        return jnp.concatenate(
            [lax.dynamic_slice_in_dim(full, XW * t, XW, full.ndim - 1), full[..., DSSM:]], -1
        )

    weights = []
    for layer in range(LAYERS):
        part = [
            small_all[:, layer, offsets[i] : offsets[i + 1]].astype(F32) for i in range(len(sizes))
        ]
        cw = part[1].reshape(fs, CONV, -1).transpose(1, 0, 2).reshape(CONV, CONVCH)
        full = [p.reshape(-1) for p in part]
        weights.append(
            dict(
                w1=w1[layer],
                w2=w2[layer],
                wr=wr[layer],
                norm_gain=full[0],
                conv_weight=own_conv(cw),
                conv_bias=own_conv(full[2]),
                dt_bias=lax.dynamic_slice_in_dim(full[3], HEADS * t, HEADS, 0),
                decay_log=lax.dynamic_slice_in_dim(full[4], HEADS * t, HEADS, 0),
                skip_gain=lax.dynamic_slice_in_dim(full[5], HEADS * t, HEADS, 0),
                mixer_gain=lax.dynamic_slice_in_dim(full[6], XW * t, XW, 0),
                ffn_gain=full[7],
            )
        )

    h = dot(to_seq, x_all)
    saved = []
    for layer in range(LAYERS):
        mid, act, kept = layer_forward(h, weights[layer], meta)
        saved.append(kept)
        if layer < LAYERS - 1:
            h = mid + lax.psum(dot(act, weights[layer]["wr"][XW + HD :]).astype(BF), TPA).astype(F32)

    own_place = lax.dynamic_slice_in_dim(place, (rep * TP + t) * own_rows, own_rows, 0)
    own_hot = one_hot(own_place, rows)
    rep_place = lax.dynamic_slice_in_dim(place, rep * TP * own_rows, TP * own_rows, 0)
    act_rep = dot(one_hot(rep_place, rows), act).astype(BF)
    down_own = lax.psum_scatter(
        dot(act_rep, weights[-1]["wr"][XW + HD :]).astype(BF), TPA, scatter_dimension=0, tiled=True
    )
    mid_own = jnp.dot(
        own_hot.astype(F32), mid, precision=lax.Precision.HIGHEST, preferred_element_type=F32
    )
    block_out = (mid_own + down_own.astype(F32)).astype(BF)

    gout = dot(to_seq, g_all)
    big = [None, None]
    small = [None, None]
    for layer in reversed(range(LAYERS)):
        gout, grads, small_grads = layer_backward(gout, weights[layer], saved[layer], meta)
        d_w1, d_w2, d_wr, d_down = grads
        col_2 = lax.psum_scatter(d_w2.astype(BF), "fsdp", scatter_dimension=0, tiled=True)
        d_rows = jnp.concatenate([d_wr.astype(BF), d_down.astype(BF)], 0)
        d_rows = lax.ppermute(d_rows, axes, back)
        d_rows = lax.psum_scatter(d_rows, "zz", scatter_dimension=0, tiled=True)
        col_1 = lax.psum_scatter(d_w1.astype(BF), "fsdp", scatter_dimension=0, tiled=True)
        big[layer] = (
            lax.all_gather(col_1, TPA, axis=0),
            lax.all_gather(col_2, TPA, axis=0),
            lax.all_gather(d_rows, TPA, axis=0),
        )
        small[layer] = small_grads
    in_grad = dot(own_hot, gout.astype(BF)).astype(BF)

    first = (t == 0).astype(F32)

    def spread_conv(vec):
        zero = jnp.zeros(vec.shape[:-1] + (DSSM,), F32)
        at = (0,) * (vec.ndim - 1) + (XW * t,)
        return jnp.concatenate(
            [lax.dynamic_update_slice(zero, vec[..., :XW], at), vec[..., XW:]], -1
        )

    def spread(vec, count):
        return lax.dynamic_update_slice(jnp.zeros((count,), F32), vec, (vec.shape[0] * t,))

    flat = []
    for layer in range(LAYERS):
        g_n, g_cw, g_cb, g_db, g_dl, g_sk, g_mg, g_fg = small[layer]
        flat += [
            g_n * first,
            spread_conv(g_cw).T.reshape(-1),
            spread_conv(g_cb),
            spread(g_db, MH),
            spread(g_dl, MH),
            spread(g_sk, MH),
            spread(g_mg, DSSM),
            g_fg * first,
        ]
    summed = lax.psum(jnp.concatenate(flat), ("fsdp",) + TPA)
    full_sizes = [fs * s for s in sizes] * LAYERS
    outs_small = [[] for _ in sizes]
    at = 0
    for i, size in enumerate(full_sizes):
        own = size // fs
        outs_small[i % len(sizes)].append(lax.dynamic_slice_in_dim(summed, at + own * f, own, 0))
        at += size
    (o_norm, o_cw, o_cb, o_db, o_dl, o_sk, o_mg, o_fg) = [jnp.stack(o) for o in outs_small]
    o_cw = o_cw.reshape(LAYERS, -1, CONV)

    def joined(parts):
        return parts.transpose(1, 0, 2).reshape(parts.shape[1], -1)

    o_in, o_q, o_k, o_v, o_gate, o_up, o_out, o_attn, o_down = [[] for _ in range(9)]
    for layer in range(LAYERS):
        c1, c2, rw = big[layer]
        c1 = c1.astype(F32)
        c2 = c2.astype(F32)
        bc = jnp.sum(c1[:, :, 2 * XW : XW + CW], axis=0)
        o_in.append(
            jnp.concatenate(
                [
                    joined(c1[:, :, :XW]),
                    joined(c1[:, :, XW : 2 * XW]),
                    bc,
                    joined(c1[:, :, XW + CW : XW + CW + HEADS]),
                ],
                1,
            )
        )
        o_q.append(joined(c1[:, :, 768:896]))
        group = TP // KVH
        o_k.append(joined(jnp.sum(c1[:, :, 896:1024].reshape(KVH, group, -1, HD), axis=1)))
        o_v.append(joined(jnp.sum(c1[:, :, 1024:1152].reshape(KVH, group, -1, HD), axis=1)))
        o_gate.append(joined(c2[:, :, :ff]))
        o_up.append(joined(c2[:, :, ff:]))
        rw = rw.astype(F32).reshape(ZZ, PAR, -1, width).transpose(1, 0, 2, 3)
        rw = rw.reshape(PAR, -1, width)
        o_out.append(rw[:, :XW].reshape(-1, width))
        o_attn.append(rw[:, XW : XW + HD].reshape(-1, width))
        o_down.append(rw[:, XW + HD :].reshape(-1, width))

    return (
        block_out,
        in_grad,
        o_norm,
        jnp.stack(o_in),
        o_cw,
        o_cb,
        o_db,
        o_dl,
        o_sk,
        o_mg,
        jnp.stack(o_out),
        jnp.stack(o_q),
        jnp.stack(o_k),
        jnp.stack(o_v),
        jnp.stack(o_attn),
        o_fg,
        jnp.stack(o_gate),
        jnp.stack(o_up),
        jnp.stack(o_down),
    )


def solution(mesh):
    fs = mesh.shape["fsdp"]
    inner = Mesh(
        mesh.devices.reshape(fs, mesh.shape["ctx"] // TP, ZZ, PAR), ("fsdp", "rep", "zz", "par")
    )
    tokens = P(("fsdp", "rep", "zz", "par"), None)
    vec = P(None, "fsdp")
    mat = P(None, "fsdp", None)
    kinds = (
        vec, mat, mat, vec, vec, vec, vec, vec, mat, mat, mat, mat, mat, vec, mat, mat, mat
    )
    return jax.shard_map(
        per_device,
        mesh=inner,
        in_specs=(tokens, P("fsdp", None)) + kinds + (tokens,),
        out_specs=(tokens, tokens) + kinds,
        check_vma=False,
    )
```

```python
import math

import jax
import jax.numpy as jnp
from jax import lax
from jax.sharding import Mesh, PartitionSpec as P

QH = 8
KVH = 2
HD = 128
MH = 24
MP = 64
NS = 128
CONV = 4
LAYERS = 2
SEQS = 3
DSSM = 1536
CONVCH = 1792
TP = 8
ZZ = 4
PAR = 2
HEADS = MH // TP
XW = HEADS * MP
CW = XW + 2 * NS
CHUNK = 128

EPSILON = 1e-05
ROPE_BASE = 100000000000.0
MASKED = -1e30
BF = jnp.bfloat16
F32 = jnp.float32
TPA = ("zz", "par")


def dot(a, b):
    return jnp.dot(a, b, preferred_element_type=F32)


def dot_nt(a, b):
    return lax.dot_general(a, b, (((1,), (1,)), ((), ())), preferred_element_type=F32)


def dot_tn(a, b):
    return lax.dot_general(a, b, (((0,), (0,)), ((), ())), preferred_element_type=F32)


def rotate(vectors, cosine, sine):
    half = HD // 2
    a = vectors[:, :half]
    b = vectors[:, half:]
    return jnp.concatenate([a * cosine - b * sine, b * cosine + a * sine], axis=-1)


def one_hot(index, count):
    return (index[:, None] == jnp.arange(count, dtype=jnp.int32)[None, :]).astype(BF)


def swapped(shard, axis, by):
    size = lax.axis_size(axis)
    return lax.ppermute(shard, axis, [(i, i ^ by) for i in range(size)])


def tp_sum(values):
    values = values + swapped(values, "par", 1)
    others = [swapped(values, "zz", by) for by in range(1, ZZ)]
    for other in others:
        values = values + other
    return values


def gathered_rows(shard, axis):
    size, own = lax.axis_size(axis), lax.axis_index(axis)
    rows = shard.shape[0]
    whole = jnp.zeros((size * rows,) + shard.shape[1:], shard.dtype)
    others = [swapped(shard, axis, by) for by in range(1, size)]
    for by, block in enumerate([shard] + others):
        whole = lax.dynamic_update_slice_in_dim(whole, block, (own ^ by) * rows, 0)
    return whole


def scattered_rows(whole, axis):
    size, own = lax.axis_size(axis), lax.axis_index(axis)
    rows = whole.shape[0] // size
    blocks = [
        lax.dynamic_slice_in_dim(whole, (own ^ by) * rows, rows, 0) for by in range(size)
    ]
    total = blocks[0].astype(F32)
    for by in range(1, size):
        total = total + swapped(blocks[by], axis, by).astype(F32)
    return total


def group_tokens(shard):
    line = [shard] + [swapped(shard, "zz", by) for by in range(1, ZZ)]
    line = jnp.concatenate(line, 0)
    both = jnp.concatenate([line, swapped(line, "par", 1)], 0)
    if lax.axis_size("rep") > 1:
        both = lax.all_gather(both, "rep", axis=0, tiled=True)
    return both


def inv_rms(values):
    return lax.rsqrt(jnp.mean(values * values, axis=-1, keepdims=True) + EPSILON)


def rms_back(grad_y, values, inv, gain):
    scaled = values * inv
    gg = grad_y * gain
    grad_v = (gg - scaled * jnp.mean(gg * scaled, axis=-1, keepdims=True)) * inv
    grad_g = jnp.sum(grad_y * scaled, axis=0)
    return grad_v, grad_g


def ssd_local(conv_in, dt_raw, conv_weight, conv_bias, dt_bias, decay_log, skip_gain, seg, pos):
    rows = conv_in.shape[0]
    conv_sum = conv_bias[None, :] + conv_weight[CONV - 1][None, :] * conv_in
    for lag in range(1, CONV):
        shifted = jnp.concatenate(
            [jnp.zeros((lag, CW), conv_in.dtype), conv_in[: rows - lag]], axis=0
        )
        conv_sum = conv_sum + conv_weight[CONV - 1 - lag][None, :] * jnp.where(
            (pos >= lag)[:, None], shifted, 0.0
        )
    conv_out = jax.nn.silu(conv_sum)
    rounded = lax.optimization_barrier(conv_out.astype(BF)).astype(F32)
    conv_out = conv_out + lax.stop_gradient(rounded - conv_out)
    chunks = rows // CHUNK
    xs = conv_out[:, :XW].reshape(chunks, CHUNK, HEADS, MP)
    bm = conv_out[:, XW : XW + NS].reshape(chunks, CHUNK, NS)
    cm = conv_out[:, XW + NS :].reshape(chunks, CHUNK, NS)
    dt = jax.nn.softplus(dt_raw + dt_bias[None, :]).reshape(chunks, CHUNK, HEADS)
    la = -dt * jnp.exp(decay_log)
    cum = jnp.cumsum(la, axis=1)
    sg = seg.reshape(chunks, CHUNK)
    causal = (sg[:, :, None] == sg[:, None, :]) & jnp.tril(jnp.ones((CHUNK, CHUNK), bool))[None]
    cum_t = cum.transpose(0, 2, 1)
    dt_t = dt.transpose(0, 2, 1)
    gap = jnp.where(causal[:, None], cum_t[:, :, :, None] - cum_t[:, :, None, :], MASKED)
    cb = jnp.einsum("cin,cjn->cij", cm, bm)
    kern = jnp.exp(gap) * cb[:, None] * dt_t[:, :, None, :]
    y = jnp.einsum("chij,cjhp->cihp", kern, xs)
    last = cum[:, -1, :]
    wend = (
        jnp.exp(last[:, None, :] - cum) * dt * (sg == sg[:, -1:]).astype(F32)[:, :, None]
    )
    ends = jnp.einsum("cjh,cjhp,cjn->chpn", wend, xs, bm)
    running = jnp.cumsum(last, axis=0)
    before = running - last
    ids = jnp.arange(chunks)
    seg_last = sg[:, -1]
    prev_seg = jnp.concatenate([jnp.full((1,), -1, seg_last.dtype), seg_last[:-1]])
    flows = (ids[:, None] > ids[None, :]) & (prev_seg[:, None] == seg_last[None, :])
    carry = jnp.exp(jnp.where(flows[:, :, None], before[:, None, :] - running[None, :, :], MASKED))
    state_in = jnp.einsum("cdh,dhpn->chpn", carry, ends)
    win = jnp.exp(cum) * (sg == prev_seg[:, None]).astype(F32)[:, :, None]
    y = y + jnp.einsum("cin,chpn->cihp", cm, state_in) * win[..., None]
    y = y + skip_gain[None, None, :, None] * xs
    return y.reshape(rows, XW)


def attn_block(q, k, seg_q, pos_q, seg, pos):
    scores = dot_nt(q, k) * HD ** (-0.5)
    allowed = (seg_q[:, None] == seg[None, :]) & (pos[None, :] <= pos_q[:, None])
    return jnp.where(allowed, scores, MASKED)


def in_blocks(step, carry, arrays):
    rows = arrays[0].shape[0]
    size = min(rows, 1024 * 1024 // rows)
    if size == rows:
        return step(carry, arrays)
    split = tuple(a.reshape((rows // size, size) + a.shape[1:]) for a in arrays)
    carry, outs = lax.scan(step, carry, split)
    return carry, jax.tree.map(lambda o: o.reshape((rows,) + o.shape[2:]), outs)


def attn_forward(q, k, v, seg, pos):
    def step(carry, block):
        q_b, seg_b, pos_b = block
        scores = attn_block(q_b, k, seg_b, pos_b, seg, pos)
        top = jnp.max(scores, axis=-1, keepdims=True)
        prob = jnp.exp(scores - top)
        total = jnp.sum(prob, axis=-1, keepdims=True)
        return carry, (dot(prob.astype(BF), v) / total, top + jnp.log(total))

    return in_blocks(step, 0.0, (q, seg, pos))[1]


def attn_backward(q, k, v, grad, delta, logs, seg, pos):
    def step(carry, block):
        q_b, grad_b, delta_b, logs_b, seg_b, pos_b = block
        prob = jnp.exp(attn_block(q_b, k, seg_b, pos_b, seg, pos) - logs_b)
        gs = (prob * (dot_nt(grad_b, v) - delta_b)).astype(BF)
        gk = carry[0] + dot_tn(gs, q_b) * HD ** (-0.5)
        gv = carry[1] + dot_tn(prob.astype(BF), grad_b)
        return (gk, gv), dot(gs, k) * HD ** (-0.5)

    zero = jnp.zeros(k.shape, F32)
    (gk, gv), gq = in_blocks(step, (zero, zero), (q, grad, delta, logs, seg, pos))
    return gq, gk, gv


def layer_forward(h, w, meta):
    seg, pos, cosine, sine = meta
    inv1 = inv_rms(h)
    normed = (h * inv1 * w["norm_gain"]).astype(BF)
    pr = dot(normed, w["w1"])
    proj = pr[:, :768].astype(BF)
    q = rotate(pr[:, 768:896], cosine, sine).astype(BF)
    k = rotate(pr[:, 896:1024], cosine, sine).astype(BF)
    v = pr[:, 1024:1152].astype(BF)
    z = proj[:, :XW].astype(F32)
    conv_in = proj[:, XW : XW + CW].astype(F32)
    dt_raw = proj[:, XW + CW : XW + CW + HEADS].astype(F32)

    def run(ci, dr, cw, cb, db, dl, sk):
        return ssd_local(ci, dr, cw, cb, db, dl, sk, seg, pos)

    ssd, pull = jax.vjp(
        run,
        conv_in,
        dt_raw,
        w["conv_weight"],
        w["conv_bias"],
        w["dt_bias"],
        w["decay_log"],
        w["skip_gain"],
    )
    gated = ssd * jax.nn.silu(z)
    square = tp_sum(jnp.sum(gated * gated, axis=-1))
    attended, logs = attn_forward(q, k, v, seg, pos)
    inv_g = lax.rsqrt(square / DSSM + EPSILON)[:, None]
    mixer = (gated * inv_g * w["mixer_gain"]).astype(BF)
    att_low = attended.astype(BF)
    mixed = jnp.concatenate([mixer, att_low], axis=1)
    mid = h + lax.psum(dot(mixed, w["wr"][: XW + HD]).astype(BF), TPA).astype(F32)
    inv2 = inv_rms(mid)
    normed2 = (mid * inv2 * w["ffn_gain"]).astype(BF)
    gu = dot(normed2, w["w2"])
    ff = gu.shape[1] // 2
    act = (jax.nn.silu(gu[:, :ff]) * gu[:, ff:]).astype(BF)
    kept = dict(
        h=h, inv1=inv1, normed=normed, z=z, ssd=ssd, gated=gated, pull=pull, inv_g=inv_g,
        q=q, k=k, v=v, attended=attended, logs=logs, mixed=mixed, mid=mid, inv2=inv2,
        normed2=normed2, gu=gu, act=act,
    )
    return mid, act, kept


def layer_backward(gout, w, kept, meta, reduce_rows, pending):
    seg, pos, cosine, sine = meta
    g_down = gout.astype(BF)
    g_act = dot_nt(g_down, w["wr"][XW + HD :])
    d_down = dot_tn(kept["act"], g_down)
    ff = kept["gu"].shape[1] // 2
    gate, up = kept["gu"][:, :ff], kept["gu"][:, ff:]
    sig = jax.nn.sigmoid(gate)
    g_gate = g_act * up * sig * (1.0 + gate * (1.0 - sig))
    g_up = g_act * gate * sig
    g_gu = jnp.concatenate([g_gate.astype(BF), g_up.astype(BF)], axis=1)
    g_n2 = lax.psum(dot_nt(g_gu, w["w2"]).astype(BF), TPA).astype(F32)
    d_w2 = dot_tn(kept["normed2"], g_gu)
    g_mid, d_ffn_gain = rms_back(g_n2, kept["mid"], kept["inv2"], w["ffn_gain"])
    g_mid = gout + g_mid
    g_low = g_mid.astype(BF)
    g_mixed = dot_nt(g_low, w["wr"][: XW + HD])
    d_wr = dot_tn(kept["mixed"], g_low)
    early = reduce_rows(d_w2, d_wr, d_down)
    if pending is None:
        pending = early()
    g_mix = g_mixed[:, :XW]
    scaled = kept["gated"] * kept["inv_g"]
    gg = g_mix * w["mixer_gain"]
    d_mixer_gain = jnp.sum(g_mix * scaled, axis=0)
    mean = tp_sum(jnp.sum(gg * scaled, axis=-1))[:, None] / DSSM
    g_att = g_mixed[:, XW:].astype(BF)
    delta = jnp.sum(g_att.astype(F32) * kept["attended"], axis=-1, keepdims=True)
    gq, gk, gv = attn_backward(
        kept["q"], kept["k"], kept["v"], g_att, delta, kept["logs"], seg, pos
    )
    gq = rotate(gq.astype(BF).astype(F32), cosine, -sine).astype(BF)
    gk = rotate(gk.astype(BF).astype(F32), cosine, -sine).astype(BF)
    g_gated = (gg - scaled * mean) * kept["inv_g"]
    z = kept["z"]
    sz = jax.nn.sigmoid(z)
    g_ssd = g_gated * z * sz
    g_z = g_gated * kept["ssd"] * sz * (1.0 + z * (1.0 - sz))
    g_conv, g_dt, d_cw, d_cb, d_db, d_dl, d_sk = kept["pull"](g_ssd)
    rows = gout.shape[0]
    g_pr = jnp.concatenate(
        [
            g_z.astype(BF),
            g_conv.astype(BF),
            g_dt.astype(BF),
            jnp.zeros((rows, 128 - HEADS), BF),
            gq,
            gk,
            gv.astype(BF),
        ],
        axis=1,
    )
    g_pr, pending = lax.optimization_barrier((g_pr, pending))
    g_n1 = lax.psum(dot_nt(g_pr, w["w1"]).astype(BF), TPA).astype(F32)
    d_w1 = dot_tn(kept["normed"], g_pr)
    g_h, d_norm_gain = rms_back(g_n1, kept["h"], kept["inv1"], w["norm_gain"])
    small = (d_norm_gain, d_cw, d_cb, d_db, d_dl, d_sk, d_mixer_gain, d_ffn_gain)
    return g_mid + g_h, d_w1, early, pending, small


def per_device(
    block_in,
    seq_lengths,
    norm_gain,
    in_proj,
    conv_weight,
    conv_bias,
    dt_bias,
    decay_log,
    skip_gain,
    mixer_gain,
    out_proj,
    query_proj,
    key_proj,
    value_proj,
    attn_proj,
    ffn_gain,
    gate_proj,
    up_proj,
    down_proj,
    out_grad,
):
    fs = lax.axis_size("fsdp")
    reps = lax.axis_size("rep")
    ctx = reps * TP
    own_rows, width = block_in.shape
    rows = ctx * own_rows
    f = lax.axis_index("fsdp")
    rep = lax.axis_index("rep")
    t = lax.axis_index(TPA)
    every = ("rep",) + TPA

    lengths = seq_lengths[0]
    ends = jnp.cumsum(lengths)
    starts = ends - lengths
    line = jnp.arange(rows, dtype=jnp.int32)
    seg = jnp.sum((line[:, None] >= ends[None, :]).astype(jnp.int32), axis=1)
    pos = line - jnp.sum(jnp.where(seg[:, None] == jnp.arange(SEQS)[None, :], starts[None, :], 0), axis=1)
    pieces = lengths // ctx
    p_ends = jnp.cumsum(pieces)
    p_starts = p_ends - pieces
    local = line % own_rows
    piece = line // own_rows
    l_seg = jnp.sum((local[:, None] >= p_ends[None, :]).astype(jnp.int32), axis=1)
    pick = l_seg[:, None] == jnp.arange(SEQS)[None, :]
    place = (
        jnp.sum(jnp.where(pick, starts[None, :] - p_starts[None, :] + piece[:, None] * pieces[None, :], 0), axis=1)
        + local
    )
    zz = lax.axis_index("zz")
    slot = jnp.arange(ctx, dtype=jnp.int32)
    near = (zz ^ (slot % ZZ)) * PAR + (lax.axis_index("par") ^ (slot // ZZ % PAR))
    order = (slot // TP * TP + near)[:, None] * own_rows
    order = (order + jnp.arange(own_rows, dtype=jnp.int32)[None, :]).reshape(-1)
    place_rel = place[order]
    half = HD // 2
    frequency = jnp.exp(-math.log(ROPE_BASE) * jnp.arange(half, dtype=F32) / half)
    angles = pos.astype(F32)[:, None] * frequency[None, :]
    meta = (seg, pos, jnp.cos(angles), jnp.sin(angles))

    to_seq = one_hot(place_rel, rows).T
    x_all = group_tokens(block_in)

    def columns(layer):
        pieces_1 = [
            lax.dynamic_slice_in_dim(in_proj[layer], XW * t, XW, 1),
            lax.dynamic_slice_in_dim(in_proj[layer], DSSM + XW * t, XW, 1),
            in_proj[layer][:, 2 * DSSM : DSSM + CONVCH],
            lax.dynamic_slice_in_dim(in_proj[layer], DSSM + CONVCH + HEADS * t, HEADS, 1),
            jnp.zeros((in_proj.shape[1], 128 - HEADS), BF),
            lax.dynamic_slice_in_dim(query_proj[layer], HD * t, HD, 1),
            lax.dynamic_slice_in_dim(key_proj[layer], HD * (t * KVH // TP), HD, 1),
            lax.dynamic_slice_in_dim(value_proj[layer], HD * (t * KVH // TP), HD, 1),
        ]
        ff = gate_proj.shape[2] // TP
        pieces_2 = [
            lax.dynamic_slice_in_dim(gate_proj[layer], ff * t, ff, 1),
            lax.dynamic_slice_in_dim(up_proj[layer], ff * t, ff, 1),
        ]
        return jnp.concatenate(pieces_1, 1), jnp.concatenate(pieces_2, 1)

    par = t % PAR
    ff = gate_proj.shape[2] // TP

    def row_pieces(layer):
        return jnp.concatenate(
            [
                lax.dynamic_slice_in_dim(out_proj[layer], XW * par, XW, 0),
                lax.dynamic_slice_in_dim(attn_proj[layer], HD * par, HD, 0),
                lax.dynamic_slice_in_dim(down_proj[layer], ff * par, ff, 0),
            ],
            0,
        )

    forth = []
    for s in range(fs):
        for r in range(reps):
            for c in range(TP):
                src = (s * reps + r) * TP + c
                dst = ((c // PAR) * reps + r) * TP + PAR * s + c % PAR
                forth.append((src, dst))
    back = [(b, a) for a, b in forth]
    axes = ("fsdp",) + every

    smalls = jnp.concatenate(
        [
            norm_gain,
            conv_weight.transpose(0, 2, 1).reshape(LAYERS, -1),
            conv_bias,
            dt_bias,
            decay_log,
            skip_gain,
            mixer_gain,
            ffn_gain,
        ],
        axis=1,
    )
    small_all = lax.all_gather(smalls, "fsdp", axis=0)
    w1_own, w2_own = zip(*[columns(layer) for layer in range(LAYERS)])
    w1 = [None, None]
    w2 = [None, None]
    wr = [None, None]
    for layer in range(LAYERS):
        w1[layer] = gathered_rows(w1_own[layer], "fsdp")
        wr[layer] = lax.ppermute(row_pieces(layer), axes, forth)
        w2[layer] = gathered_rows(w2_own[layer], "fsdp")
    g_all = group_tokens(out_grad)

    sizes = [
        norm_gain.shape[1],
        CONV * conv_weight.shape[1],
        conv_bias.shape[1],
        dt_bias.shape[1],
        decay_log.shape[1],
        skip_gain.shape[1],
        mixer_gain.shape[1],
        ffn_gain.shape[1],
    ]
    offsets = [sum(sizes[:i]) for i in range(len(sizes) + 1)]

    def own_conv(full):
        return jnp.concatenate(
            [lax.dynamic_slice_in_dim(full, XW * t, XW, full.ndim - 1), full[..., DSSM:]], -1
        )

    weights = []
    for layer in range(LAYERS):
        part = [
            small_all[:, layer, offsets[i] : offsets[i + 1]].astype(F32) for i in range(len(sizes))
        ]
        cw = part[1].reshape(fs, CONV, -1).transpose(1, 0, 2).reshape(CONV, CONVCH)
        full = [p.reshape(-1) for p in part]
        weights.append(
            dict(
                w1=w1[layer],
                w2=w2[layer],
                wr=wr[layer],
                norm_gain=full[0],
                conv_weight=own_conv(cw),
                conv_bias=own_conv(full[2]),
                dt_bias=lax.dynamic_slice_in_dim(full[3], HEADS * t, HEADS, 0),
                decay_log=lax.dynamic_slice_in_dim(full[4], HEADS * t, HEADS, 0),
                skip_gain=lax.dynamic_slice_in_dim(full[5], HEADS * t, HEADS, 0),
                mixer_gain=lax.dynamic_slice_in_dim(full[6], XW * t, XW, 0),
                ffn_gain=full[7],
            )
        )

    h = dot(to_seq, x_all)
    saved = []
    for layer in range(LAYERS):
        mid, act, kept = layer_forward(h, weights[layer], meta)
        saved.append(kept)
        if layer < LAYERS - 1:
            h = mid + lax.psum(dot(act, weights[layer]["wr"][XW + HD :]).astype(BF), TPA).astype(F32)

    own_place = lax.dynamic_slice_in_dim(place, (rep * TP + t) * own_rows, own_rows, 0)
    own_hot = one_hot(own_place, rows)
    rep_place = lax.dynamic_slice_in_dim(place, rep * TP * own_rows, TP * own_rows, 0)
    act_rep = dot(one_hot(rep_place, rows), act).astype(BF)
    down_own = lax.psum_scatter(
        dot(act_rep, weights[-1]["wr"][XW + HD :]).astype(BF), TPA, scatter_dimension=0, tiled=True
    )
    mid_own = jnp.dot(
        own_hot.astype(F32), mid, precision=lax.Precision.HIGHEST, preferred_element_type=F32
    )
    block_out = (mid_own + down_own.astype(F32)).astype(BF)

    gout = dot(to_seq, g_all)
    big = [None, None]

    def reduce_rows(d_w2, d_wr, d_down):
        d_rows = jnp.concatenate([d_wr.astype(BF), d_down.astype(BF)], 0)
        d_rows = scattered_rows(lax.ppermute(d_rows, axes, back), "zz").astype(BF)
        part = jnp.concatenate(
            [
                scattered_rows(d_w2.astype(BF), "fsdp").astype(BF),
                d_rows.reshape(d_w2.shape[0] // fs, -1),
            ],
            1,
        )
        return lambda: lax.all_gather(part, TPA, axis=0)

    def reduce_columns(d_w1, small_grads):
        g_n, g_cw, g_cb, g_db, g_dl, g_sk, g_mg, g_fg = small_grads
        small = jnp.concatenate(
            [g_n, g_cw.reshape(-1), g_cb, g_db, g_dl, g_sk, g_mg, g_fg]
        )
        others = [swapped(small, "fsdp", by) for by in range(1, fs)]
        for other in others:
            small = small + other
        part = scattered_rows(d_w1.astype(BF), "fsdp").astype(BF)
        held = jnp.zeros((part.shape[0] * 64,), BF)
        held = lax.dynamic_update_slice(held, small.astype(BF), (0,)).reshape(-1, 64)
        part = jnp.concatenate([part[:, :704], held, part[:, 768:]], 1)
        return lax.all_gather(part, TPA, axis=0)

    pending = None
    for layer in reversed(range(LAYERS)):
        gout, d_w1, early, pending, small_grads = layer_backward(
            gout, weights[layer], saved[layer], meta, reduce_rows, pending
        )
        if layer == LAYERS - 1:
            first_part = pending
            pending = reduce_columns(d_w1, small_grads)
        else:
            big[layer + 1] = (first_part, pending)
            big[layer] = (early(), reduce_columns(d_w1, small_grads))
    in_grad = dot(own_hot, gout.astype(BF)).astype(BF)

    own_sizes = [width, CONV * CW, CW, HEADS, HEADS, HEADS, XW, width]
    own_at = [sum(own_sizes[:i]) for i in range(len(own_sizes) + 1)]
    outs_small = [[] for _ in sizes]

    def conv_full(parts):
        parts = parts.astype(F32)
        return jnp.concatenate(
            [
                jnp.moveaxis(parts[..., :XW], 0, -2).reshape(parts.shape[1:-1] + (DSSM,)),
                jnp.sum(parts[..., XW:], axis=0),
            ],
            -1,
        )

    for layer in range(LAYERS):
        held = big[layer][1][:, :, 704:768].reshape(TP, -1)
        parts = [held[:, own_at[i] : own_at[i + 1]] for i in range(len(own_sizes))]
        full = [
            parts[0][0].astype(F32),
            conv_full(parts[1].reshape(TP, CONV, CW)).T.reshape(-1),
            conv_full(parts[2]),
        ]
        full += [p.astype(F32).reshape(-1) for p in parts[3:7]] + [parts[7][0].astype(F32)]
        for i, vec in enumerate(full):
            own = vec.shape[0] // fs
            outs_small[i].append(lax.dynamic_slice_in_dim(vec, own * f, own, 0))
    (o_norm, o_cw, o_cb, o_db, o_dl, o_sk, o_mg, o_fg) = [jnp.stack(o) for o in outs_small]
    o_cw = o_cw.reshape(LAYERS, -1, CONV)

    def joined(parts):
        return parts.transpose(1, 0, 2).reshape(parts.shape[1], -1)

    o_in, o_q, o_k, o_v, o_gate, o_up, o_out, o_attn, o_down = [[] for _ in range(9)]
    for layer in range(LAYERS):
        c2, c1 = big[layer]
        rw = c2[:, :, 2 * ff :].reshape(TP, -1, width)
        c1 = c1.astype(F32)
        c2 = c2.astype(F32)
        bc = jnp.sum(c1[:, :, 2 * XW : XW + CW], axis=0)
        o_in.append(
            jnp.concatenate(
                [
                    joined(c1[:, :, :XW]),
                    joined(c1[:, :, XW : 2 * XW]),
                    bc,
                    joined(c1[:, :, XW + CW : XW + CW + HEADS]),
                ],
                1,
            )
        )
        o_q.append(joined(c1[:, :, 768:896]))
        group = TP // KVH
        o_k.append(joined(jnp.sum(c1[:, :, 896:1024].reshape(KVH, group, -1, HD), axis=1)))
        o_v.append(joined(jnp.sum(c1[:, :, 1024:1152].reshape(KVH, group, -1, HD), axis=1)))
        o_gate.append(joined(c2[:, :, :ff]))
        o_up.append(joined(c2[:, :, ff : 2 * ff]))
        rw = rw.astype(F32).reshape(ZZ, PAR, -1, width).transpose(1, 0, 2, 3)
        rw = rw.reshape(PAR, -1, width)
        o_out.append(rw[:, :XW].reshape(-1, width))
        o_attn.append(rw[:, XW : XW + HD].reshape(-1, width))
        o_down.append(rw[:, XW + HD :].reshape(-1, width))

    return (
        block_out,
        in_grad,
        o_norm,
        jnp.stack(o_in),
        o_cw,
        o_cb,
        o_db,
        o_dl,
        o_sk,
        o_mg,
        jnp.stack(o_out),
        jnp.stack(o_q),
        jnp.stack(o_k),
        jnp.stack(o_v),
        jnp.stack(o_attn),
        o_fg,
        jnp.stack(o_gate),
        jnp.stack(o_up),
        jnp.stack(o_down),
    )


def solution(mesh):
    fs = mesh.shape["fsdp"]
    inner = Mesh(
        mesh.devices.reshape(fs, mesh.shape["ctx"] // TP, ZZ, PAR), ("fsdp", "rep", "zz", "par")
    )
    tokens = P(("fsdp", "rep", "zz", "par"), None)
    vec = P(None, "fsdp")
    mat = P(None, "fsdp", None)
    kinds = (
        vec, mat, mat, vec, vec, vec, vec, vec, mat, mat, mat, mat, mat, vec, mat, mat, mat
    )
    return jax.shard_map(
        per_device,
        mesh=inner,
        in_specs=(tokens, P("fsdp", None)) + kinds + (tokens,),
        out_specs=(tokens, tokens) + kinds,
        check_vma=False,
    )
```

```python
import math

import jax
import jax.numpy as jnp
from jax import lax
from jax.experimental import pallas as pl
from jax.experimental.pallas import tpu as pltpu
from jax.sharding import Mesh, PartitionSpec as P

QH = 8
KVH = 2
HD = 128
MH = 24
MP = 64
NS = 128
CONV = 4
LAYERS = 2
SEQS = 3
DSSM = 1536
CONVCH = 1792
TP = 8
ZZ = 4
PAR = 2
HEADS = MH // TP
XW = HEADS * MP
CW = XW + 2 * NS
CHUNK = 256
ATTN = 256
DTL = 64

EPSILON = 1e-05
ROPE_BASE = 100000000000.0
MASKED = -1e30
BF = jnp.bfloat16
F32 = jnp.float32
TPA = ("zz", "par")


def dot(a, b):
    return jnp.dot(a, b, preferred_element_type=F32)


def dot_nt(a, b):
    return lax.dot_general(a, b, (((1,), (1,)), ((), ())), preferred_element_type=F32)


def dot_tn(a, b):
    return lax.dot_general(a, b, (((0,), (0,)), ((), ())), preferred_element_type=F32)


def one_hot(index, count):
    return (index[:, None] == jnp.arange(count, dtype=jnp.int32)[None, :]).astype(BF)


def swapped(shard, axis, by):
    size = lax.axis_size(axis)
    return lax.ppermute(shard, axis, [(i, i ^ by) for i in range(size)])


def tp_sum(values):
    values = values + swapped(values, "par", 1)
    others = [swapped(values, "zz", by) for by in range(1, ZZ)]
    for other in others:
        values = values + other
    return values


def gathered_rows(shard, axis):
    size, own = lax.axis_size(axis), lax.axis_index(axis)
    rows = shard.shape[0]
    whole = jnp.zeros((size * rows,) + shard.shape[1:], shard.dtype)
    others = [swapped(shard, axis, by) for by in range(1, size)]
    for by, block in enumerate([shard] + others):
        whole = lax.dynamic_update_slice_in_dim(whole, block, (own ^ by) * rows, 0)
    return whole


def scattered_rows(whole, axis):
    size, own = lax.axis_size(axis), lax.axis_index(axis)
    rows = whole.shape[0] // size
    blocks = [
        lax.dynamic_slice_in_dim(whole, (own ^ by) * rows, rows, 0) for by in range(size)
    ]
    total = blocks[0].astype(F32)
    for by in range(1, size):
        total = total + swapped(blocks[by], axis, by).astype(F32)
    return total


def group_tokens(shard):
    line = [shard] + [swapped(shard, "zz", by) for by in range(1, ZZ)]
    line = jnp.concatenate(line, 0)
    both = jnp.concatenate([line, swapped(line, "par", 1)], 0)
    if lax.axis_size("rep") > 1:
        both = lax.all_gather(both, "rep", axis=0, tiled=True)
    return both


def inv_rms(values):
    return lax.rsqrt(jnp.mean(values * values, axis=-1, keepdims=True) + EPSILON)


def rms_back(grad_y, values, inv, gain):
    scaled = values * inv
    gg = grad_y * gain
    return (gg - scaled * jnp.mean(gg * scaled, axis=-1, keepdims=True)) * inv


def gain_back(grad_y, values, inv):
    return jnp.sum(grad_y.astype(F32) * (values * inv), axis=0)


def iota(shape, dim):
    return lax.broadcasted_iota(jnp.int32, shape, dim)


def exact(a, b):
    return jnp.dot(a, b, preferred_element_type=F32, precision=lax.Precision.HIGHEST)


def halves(vals):
    high = vals.astype(BF)
    return high, (vals - high.astype(F32)).astype(BF)


def fine_left(kind, a, b):
    high, low = halves(a)
    return kind(high, b) + kind(low, b)


def fine_right(kind, a, b):
    high, low = halves(b)
    return kind(a, high) + kind(a, low)


def fine_both(kind, a, b):
    a_high, a_low = halves(a)
    b_high, b_low = halves(b)
    return kind(a_high, b_high) + (kind(a_high, b_low) + kind(a_low, b_high))


def by_head(vals):
    lane = iota((1, XW), 1)
    cols = [vals[:, DTL + h : DTL + h + 1] for h in range(HEADS)]
    out = cols[HEADS - 1]
    for h in range(HEADS - 2, -1, -1):
        out = jnp.where(lane < MP * (h + 1), cols[h], out)
    return out


def head_lanes():
    return (iota((XW, 128), 0) // MP + DTL == iota((XW, 128), 1)).astype(F32)


def head_only(vals, h):
    lane = iota((1, XW), 1)
    return jnp.where((lane >= MP * h) & (lane < MP * (h + 1)), vals, 0.0)


def chunk_terms(buf, tile, meta, seg_row, taps, heads, size):
    shifts = [buf[8 : 8 + size, :]]
    for lag in range(1, CONV):
        shifts.append(buf[8 - lag : 8 - lag + size, :] * meta[:, 2 + lag : 3 + lag])
    pre = taps[CONV : CONV + 1, :] + taps[CONV - 1 : CONV, :] * shifts[0]
    for lag in range(1, CONV):
        pre = pre + taps[CONV - 1 - lag : CONV - lag, :] * shifts[lag]
    sig = jax.nn.sigmoid(pre)
    conv = (pre * sig).astype(BF)
    bm, cm, xs = conv[:, :NS], conv[:, NS : 2 * NS], conv[:, 2 * NS : CW]
    raw = tile + heads[0:1, :]
    dt = jnp.maximum(raw, 0.0) + jnp.log1p(jnp.exp(-jnp.abs(raw)))
    la = -dt * heads[1:2, :]
    row, col = iota((size, size), 0), iota((size, size), 1)
    cum = exact((row >= col).astype(F32), la)
    allowed = (meta[:, 0:1] == seg_row) & (row >= col)
    last = cum[size - 1 : size, :]
    win = jnp.exp(cum) * meta[:, 1:2]
    ramp = jnp.exp(last - cum) * meta[:, 2:3]
    flow = jnp.exp(last) * meta[size - 1 : size, 1:2]
    return dict(
        shifts=shifts, pre=pre, sig=sig, bm=bm, cm=cm, xs=xs, raw=raw, dt=dt, la=la, cum=cum,
        cum_t=cum.T, dt_t=dt.T, allowed=allowed, win=win, ramp=ramp, flow=flow,
        cb=dot_nt(cm, bm), row=row, col=col,
    )


def decay_of(t, h):
    at = DTL + h
    gap = t["cum"][:, at : at + 1] - t["cum_t"][at : at + 1, :]
    return jnp.exp(jnp.where(t["allowed"], gap, MASKED))


def ssd_fwd_kernel(
    p_ref, meta_ref, seg_ref, taps_ref, heads_ref, skip_ref, ssd_ref, gated_ref, sum_ref, st_ref,
    state, buf,
):
    size = p_ref.shape[0]

    @pl.when(pl.program_id(0) == 0)
    def _():
        state[...] = jnp.zeros_like(state)
        buf[...] = jnp.zeros_like(buf)

    st_ref[0] = state[...]
    buf[0:8, :] = buf[size : size + 8, :]
    buf[8 : 8 + size, :] = p_ref[:, :CW].astype(BF).astype(F32)
    tile = p_ref[:, 640:768].astype(BF).astype(F32)
    t = chunk_terms(buf, tile, meta_ref[...], seg_ref[0], taps_ref[...], heads_ref[...], size)
    xs = t["xs"].astype(F32)
    y = fine_right(dot_nt, t["cm"], state[...]) * by_head(t["win"]) + skip_ref[...] * xs
    for h in range(HEADS):
        at = DTL + h
        kern = decay_of(t, h) * t["cb"] * t["dt_t"][at : at + 1, :]
        y = y + fine_left(dot, kern, head_only(xs, h).astype(BF))
    weighted = xs * by_head(t["ramp"] * t["dt"])
    flow = jnp.sum(head_lanes() * t["flow"], axis=1, keepdims=True)
    state[...] = flow * state[...] + fine_left(dot_tn, weighted, t["bm"])
    z = p_ref[:, 512 : 512 + XW].astype(BF).astype(F32)
    gated = y * (z * jax.nn.sigmoid(z))
    ssd_ref[...] = y
    gated_ref[...] = gated
    ones = jnp.ones((8, XW), F32)
    total = lax.dot_general(
        ones, gated * gated, (((1,), (1,)), ((), ())), preferred_element_type=F32,
        precision=lax.Precision.HIGHEST,
    )
    sum_ref[0] = total[0:1, :]


def ssd_bwd_kernel(
    p_ref, prev_ref, meta_ref, seg_ref, ssd_ref, gmix_ref, scale_ref, st_ref, taps_ref, heads_ref,
    skip_ref, gain_ref, out_ref, taps_acc, small_acc, grad, buf, gbuf,
):
    size = p_ref.shape[0]

    @pl.when(pl.program_id(0) == 0)
    def _():
        grad[...] = jnp.zeros_like(grad)
        gbuf[...] = jnp.zeros_like(gbuf)
        taps_acc[...] = jnp.zeros_like(taps_acc)
        small_acc[...] = jnp.zeros_like(small_acc)

    buf[0:8, :] = prev_ref[:, :CW].astype(BF).astype(F32)
    buf[8 : 8 + size, :] = p_ref[:, :CW].astype(BF).astype(F32)
    tile = p_ref[:, 640:768].astype(BF).astype(F32)
    meta, taps, heads, skip = meta_ref[...], taps_ref[...], heads_ref[...], skip_ref[...]
    t = chunk_terms(buf, tile, meta, seg_ref[0], taps, heads, size)
    xs = t["xs"].astype(F32)
    z = p_ref[:, 512 : 512 + XW].astype(BF).astype(F32)
    sz = jax.nn.sigmoid(z)
    silu = z * sz
    ssd = ssd_ref[...]
    inv, mean = scale_ref[:, 0:1], scale_ref[:, 1:2]
    scaled = ssd * silu * inv
    gmix = gmix_ref[:, :XW]
    g_gated = (gmix * gain_ref[...] - scaled * mean) * inv
    gy = g_gated * silu
    gz = g_gated * ssd * sz * (1.0 + z * (1.0 - sz))
    entering = st_ref[0]
    win, ramp, dt = by_head(t["win"]), by_head(t["ramp"]), by_head(t["dt"])
    from_b = fine_right(dot_nt, t["bm"], grad[...])
    gyw = gy * win
    xw = xs * ramp * dt
    dxs = skip * gy + ramp * dt * from_b
    dc = fine_both(dot, gyw, entering)
    db = fine_both(dot, xw, grad[...])
    lanes = head_lanes()
    carried = exact(gyw * fine_right(dot_nt, t["cm"], entering), lanes)
    ramped = exact(xs * from_b * ramp, lanes)
    flow = jnp.sum(lanes * t["flow"], axis=1, keepdims=True)
    passed = jnp.sum(grad[...] * entering, axis=1, keepdims=True) * flow
    d_last = jnp.sum(lanes * passed, axis=0, keepdims=True)
    grad[...] = flow * grad[...] + fine_left(dot_tn, gyw, t["cm"])
    lane = iota((size, 128), 1)
    sub = iota((128, size), 0)
    dcb = jnp.zeros((size, size), F32)
    rows = jnp.zeros((size, 128), F32)
    cols = jnp.zeros((128, size), F32)
    for h in range(HEADS):
        at = DTL + h
        decay = decay_of(t, h)
        dt_row = t["dt_t"][at : at + 1, :]
        weight = decay * dt_row
        gy_h = head_only(gy, h)
        dk = fine_left(dot_nt, gy_h, t["xs"])
        dcb = dcb + dk * weight
        inner = dk * decay * t["cb"]
        rows = jnp.where(lane == at, jnp.sum(inner * dt_row, axis=1, keepdims=True), rows)
        cols = jnp.where(sub == at, jnp.sum(inner, axis=0, keepdims=True), cols)
        dxs = dxs + fine_both(dot_tn, weight * t["cb"], gy_h)
    cols = cols.T
    d_dt = cols + ramped
    after = ramped * t["dt"]
    d_cum = rows + carried - d_dt * t["dt"]
    d_last = d_last + jnp.sum(after, axis=0, keepdims=True)
    d_cum = d_cum + jnp.where(iota((size, 128), 0) == size - 1, d_last, 0.0)
    d_la = exact((t["row"] <= t["col"]).astype(F32), d_cum)
    d_raw = (d_dt - heads[1:2, :] * d_la) * jax.nn.sigmoid(t["raw"])
    dc = dc + fine_left(dot, dcb, t["bm"])
    db = db + fine_left(dot_tn, dcb, t["cm"])
    pre, sig = t["pre"], t["sig"]
    slope = sig * (1.0 + pre * (1.0 - sig))
    gbuf[size : size + 8, :] = gbuf[0:8, :]
    gbuf[0:size, :NS] = db * slope[:, :NS]
    gbuf[0:size, NS : 2 * NS] = dc * slope[:, NS : 2 * NS]
    gbuf[0:size, 2 * NS : CW] = dxs * slope[:, 2 * NS : CW]
    d_pre = gbuf[0:size, :]
    d_in = taps[CONV - 1 : CONV, :] * d_pre
    for lag in range(1, CONV):
        d_in = d_in + taps[CONV - 1 - lag : CONV - lag, :] * (
            gbuf[lag : lag + size, :] * meta[:, 5 + lag : 6 + lag]
        )
    for lag in range(CONV):
        at = CONV - 1 - lag
        taps_acc[at : at + 1, :] += jnp.sum(d_pre * t["shifts"][lag], axis=0, keepdims=True)
    taps_acc[CONV : CONV + 1, :] += jnp.sum(d_pre, axis=0, keepdims=True)
    small_acc[0:1, :XW] += jnp.sum(gmix * scaled, axis=0, keepdims=True)
    small_acc[1:2, :XW] += jnp.sum(gy * xs, axis=0, keepdims=True)
    small_acc[2:3, :128] += jnp.sum(d_raw, axis=0, keepdims=True)
    small_acc[3:4, :128] += jnp.sum(t["la"] * d_la, axis=0, keepdims=True)
    out_ref[:, :CW] = d_in.astype(BF)
    out_ref[:, CW:512] = jnp.zeros((size, 512 - CW), BF)
    out_ref[:, 512 : 512 + XW] = gz.astype(BF)
    out_ref[:, 704:768] = d_raw[:, DTL:].astype(BF)


def full_spec(shape):
    return pl.BlockSpec(shape, lambda i: (0,) * len(shape))


def kernel_params():
    return pltpu.CompilerParams(
        dimension_semantics=("arbitrary",), vmem_limit_bytes=48 * 1024 * 1024
    )


def ssd_forward(p, meta, seg_rows, w):
    rows = p.shape[0]
    size = min(CHUNK, rows)
    chunks = rows // size
    return pl.pallas_call(
        ssd_fwd_kernel,
        grid=(chunks,),
        in_specs=[
            pl.BlockSpec((size, 768), lambda i: (i, 0)),
            pl.BlockSpec((size, 16), lambda i: (i, 0)),
            pl.BlockSpec((1, 1, size), lambda i: (i, 0, 0)),
            full_spec((8, CW)),
            full_spec((8, 128)),
            full_spec((1, XW)),
        ],
        out_specs=[
            pl.BlockSpec((size, XW), lambda i: (i, 0)),
            pl.BlockSpec((size, XW), lambda i: (i, 0)),
            pl.BlockSpec((1, 1, size), lambda i: (i, 0, 0)),
            pl.BlockSpec((1, XW, NS), lambda i: (i, 0, 0)),
        ],
        out_shape=[
            jax.ShapeDtypeStruct((rows, XW), F32),
            jax.ShapeDtypeStruct((rows, XW), F32),
            jax.ShapeDtypeStruct((chunks, 1, size), F32),
            jax.ShapeDtypeStruct((chunks, XW, NS), F32),
        ],
        scratch_shapes=[pltpu.VMEM((XW, NS), F32), pltpu.VMEM((size + 8, CW), F32)],
        compiler_params=kernel_params(),
        cost_estimate=pl.CostEstimate(
            flops=rows * size * 2 * 1024, bytes_accessed=rows * 6000, transcendentals=rows * 1500
        ),
        name="ssd_forward",
    )(p, meta, seg_rows, w["taps"], w["heads"], w["skip"])


def ssd_backward(p, meta, seg_rows, ssd, gmix, scale, states, w):
    rows = p.shape[0]
    size = min(CHUNK, rows)
    chunks = rows // size
    back = lambda i: (chunks - 1 - i, 0)
    back3 = lambda i: (chunks - 1 - i, 0, 0)
    return pl.pallas_call(
        ssd_bwd_kernel,
        grid=(chunks,),
        in_specs=[
            pl.BlockSpec((size, 768), back),
            pl.BlockSpec(
                (8, 768), lambda i: (jnp.maximum((chunks - 1 - i) * (size // 8) - 1, 0), 0)
            ),
            pl.BlockSpec((size, 16), back),
            pl.BlockSpec((1, 1, size), back3),
            pl.BlockSpec((size, XW), back),
            pl.BlockSpec((size, XW + HD), back),
            pl.BlockSpec((size, 2), back),
            pl.BlockSpec((1, XW, NS), back3),
            full_spec((8, CW)),
            full_spec((8, 128)),
            full_spec((1, XW)),
            full_spec((1, XW)),
        ],
        out_specs=[
            pl.BlockSpec((size, 768), back),
            full_spec((8, CW)),
            full_spec((8, 256)),
        ],
        out_shape=[
            jax.ShapeDtypeStruct((rows, 1152), BF),
            jax.ShapeDtypeStruct((8, CW), F32),
            jax.ShapeDtypeStruct((8, 256), F32),
        ],
        scratch_shapes=[
            pltpu.VMEM((XW, NS), F32),
            pltpu.VMEM((size + 8, CW), F32),
            pltpu.VMEM((size + 8, CW), F32),
        ],
        compiler_params=kernel_params(),
        cost_estimate=pl.CostEstimate(
            flops=rows * size * 2 * 3000, bytes_accessed=rows * 9000, transcendentals=rows * 1500
        ),
        name="ssd_backward",
    )(p, p, meta, seg_rows, ssd, gmix, scale, states, w["taps"], w["heads"], w["skip"], w["gain"])


def turn(vals, cosine, sine):
    return vals * cosine + pltpu.roll(vals, HD // 2, 1) * sine


def allowed_keys(meta, seg_all, first):
    size, keys = meta.shape[0], seg_all.shape[1]
    return (meta[:, 0:1] == seg_all) & (iota((size, keys), 0) + first >= iota((size, keys), 1))


def attn_fwd_kernel(
    p_ref, cos_ref, sin_ref, meta_ref, seg_ref, q_ref, k_ref, v_ref, att_ref, log_ref
):
    size = q_ref.shape[0]
    first = pl.program_id(0) * size

    @pl.when(pl.program_id(0) == 0)
    def _():
        k_ref[...] = turn(p_ref[:, HD : 2 * HD], cos_ref[...], sin_ref[...]).astype(BF)
        v_ref[...] = p_ref[:, 2 * HD :].astype(BF)

    at = pl.ds(pl.multiple_of(first, size), size)
    q = turn(p_ref[at, :HD], cos_ref[at, :], sin_ref[at, :]).astype(BF)
    q_ref[...] = q
    scores = dot_nt(q, k_ref[...]) * HD ** (-0.5)
    scores = jnp.where(allowed_keys(meta_ref[...], seg_ref[...], first), scores, MASKED)
    top = jnp.max(scores, axis=1, keepdims=True)
    prob = jnp.exp(scores - top)
    total = jnp.sum(prob, axis=1, keepdims=True)
    att_ref[...] = dot(prob.astype(BF), v_ref[...]) / total
    log_ref[...] = jnp.broadcast_to(top + jnp.log(total), log_ref.shape)


def attn_bwd_kernel(
    held_ref, q_ref, k_ref, v_ref, att_ref, log_ref, g_ref, cos_ref, sin_ref, meta_ref, seg_ref,
    out_ref, gk, gv,
):
    del held_ref
    size = q_ref.shape[0]
    step = pl.program_id(0)
    first = step * size

    @pl.when(step == 0)
    def _():
        gk[...] = jnp.zeros_like(gk)
        gv[...] = jnp.zeros_like(gv)

    at = pl.ds(pl.multiple_of(first, size), size)
    q = q_ref[...]
    scores = dot_nt(q, k_ref[...]) * HD ** (-0.5) - log_ref[:, 0:1]
    keep = allowed_keys(meta_ref[...], seg_ref[...], first)
    prob = jnp.exp(jnp.where(keep, scores, MASKED))
    g = g_ref[:, XW:].astype(BF)
    delta = jnp.sum(g.astype(F32) * att_ref[...], axis=1, keepdims=True)
    gs = (prob * (dot_nt(g, v_ref[...]) - delta)).astype(BF)
    gq = (dot(gs, k_ref[...]) * HD ** (-0.5)).astype(BF).astype(F32)
    out_ref[at, :HD] = turn(gq, cos_ref[at, :], -sin_ref[at, :]).astype(BF)
    gk[...] += dot_tn(gs, q) * HD ** (-0.5)
    gv[...] += dot_tn(prob.astype(BF), g)

    @pl.when(step == pl.num_programs(0) - 1)
    def _():
        gk_low = gk[...].astype(BF).astype(F32)
        out_ref[:, HD : 2 * HD] = turn(gk_low, cos_ref[...], -sin_ref[...]).astype(BF)
        out_ref[:, 2 * HD :] = gv[...].astype(BF)


def attn_forward(p, tables, meta, seg_all):
    rows = p.shape[0]
    size = min(ATTN, rows)
    block = lambda i: (i, 0)
    return pl.pallas_call(
        attn_fwd_kernel,
        grid=(rows // size,),
        in_specs=[
            pl.BlockSpec((rows, 384), lambda i: (0, 2)),
            full_spec((rows, HD)),
            full_spec((rows, HD)),
            pl.BlockSpec((size, 16), block),
            full_spec((1, rows)),
        ],
        out_specs=[
            pl.BlockSpec((size, HD), block),
            full_spec((rows, HD)),
            full_spec((rows, HD)),
            pl.BlockSpec((size, HD), block),
            pl.BlockSpec((size, 8), block),
        ],
        out_shape=[
            jax.ShapeDtypeStruct((rows, HD), BF),
            jax.ShapeDtypeStruct((rows, HD), BF),
            jax.ShapeDtypeStruct((rows, HD), BF),
            jax.ShapeDtypeStruct((rows, HD), F32),
            jax.ShapeDtypeStruct((rows, 8), F32),
        ],
        compiler_params=kernel_params(),
        cost_estimate=pl.CostEstimate(
            flops=rows * rows * 4 * HD, bytes_accessed=rows * 4000, transcendentals=rows * rows
        ),
        name="attn_forward",
    )(p, *tables, meta, seg_all)


def attn_backward(held, q, k, v, att, logs, g_mixed, tables, meta, seg_all):
    rows = q.shape[0]
    size = min(ATTN, rows)
    block = lambda i: (i, 0)
    return pl.pallas_call(
        attn_bwd_kernel,
        grid=(rows // size,),
        in_specs=[
            pl.BlockSpec(memory_space=pl.ANY),
            pl.BlockSpec((size, HD), block),
            full_spec((rows, HD)),
            full_spec((rows, HD)),
            pl.BlockSpec((size, HD), block),
            pl.BlockSpec((size, 8), block),
            pl.BlockSpec((size, XW + HD), block),
            full_spec((rows, HD)),
            full_spec((rows, HD)),
            pl.BlockSpec((size, 16), block),
            full_spec((1, rows)),
        ],
        out_specs=pl.BlockSpec((rows, 384), lambda i: (0, 2)),
        out_shape=jax.ShapeDtypeStruct((rows, 1152), BF),
        scratch_shapes=[pltpu.VMEM((rows, HD), F32), pltpu.VMEM((rows, HD), F32)],
        input_output_aliases={0: 0},
        compiler_params=kernel_params(),
        cost_estimate=pl.CostEstimate(
            flops=rows * rows * 10 * HD, bytes_accessed=rows * 5000, transcendentals=rows * rows
        ),
        name="attn_backward",
    )(held, q, k, v, att, logs, g_mixed, *tables, meta, seg_all)


def columns_kernel(c_ref, *refs):
    in_ref, q_ref, k_ref, v_ref = refs[-4:]
    bc = None
    for t in range(TP):
        c = c_ref[t].astype(F32)
        in_ref[0, :, XW * t : XW * (t + 1)] = c[:, 512 : 512 + XW]
        in_ref[0, :, DSSM + XW * t : DSSM + XW * (t + 1)] = c[:, 2 * NS : CW]
        at = DSSM + CONVCH + HEADS * t
        in_ref[0, :, at : at + HEADS] = c[:, 704 : 704 + HEADS]
        bc = c[:, : 2 * NS] if t == 0 else bc + c[:, : 2 * NS]
        q_ref[0, :, HD * t : HD * (t + 1)] = c[:, 768:896]
        group = TP // KVH
        kv = c[:, 896:1152] if t % group == 0 else kv + c[:, 896:1152]
        if t % group == group - 1:
            at = HD * (t // group)
            k_ref[0, :, at : at + HD] = kv[:, :HD]
            v_ref[0, :, at : at + HD] = kv[:, HD:]
    in_ref[0, :, 2 * DSSM : DSSM + CONVCH] = bc


def rows_kernel(c_ref, *refs):
    gate_ref, up_ref, out_ref, attn_ref, down_ref = refs[-5:]
    ff = gate_ref.shape[2] // PAR
    for par in range(PAR):
        gate_ref[0, :, ff * par : ff * (par + 1)] = c_ref[par, :, :ff].astype(F32)
        up_ref[0, :, ff * par : ff * (par + 1)] = c_ref[par, :, ff : 2 * ff].astype(F32)
        turned = c_ref[par, :, 2 * ff :].astype(F32).T
        out_ref[0, XW * par : XW * (par + 1), :] = turned[:XW]
        attn_ref[0, HD * par : HD * (par + 1), :] = turned[XW : XW + HD]
        down_ref[0, ff * par : ff * (par + 1), :] = turned[XW + HD : XW + HD + ff]


def assembled(kernel, gathered, in_block, grid, blocks, shapes, layer, held):
    any_spec = pl.BlockSpec(memory_space=pl.ANY)
    held = () if held is None else tuple(held)
    place = [
        pl.BlockSpec((1,) + shape, lambda i, by=by: (layer,) + by(i)) for shape, by in blocks
    ]
    return pl.pallas_call(
        kernel,
        grid=(grid,),
        in_specs=[in_block] + [any_spec] * len(held),
        out_specs=place,
        out_shape=[jax.ShapeDtypeStruct((LAYERS,) + shape, F32) for shape in shapes],
        input_output_aliases={1 + i: i for i in range(len(held))},
        compiler_params=kernel_params(),
        cost_estimate=pl.CostEstimate(flops=0, bytes_accessed=12000000, transcendentals=0),
        name="assemble",
    )(gathered, *held)


def column_outputs(gathered, layer, held):
    rows = gathered.shape[1]
    size = 64
    by = lambda i: (i, 0)
    widths = (DSSM + CONVCH + MH, QH * HD, KVH * HD, KVH * HD)
    return assembled(
        columns_kernel,
        gathered,
        pl.BlockSpec((TP, size, gathered.shape[2]), lambda i: (0, i, 0)),
        rows // size,
        [((size, width), by) for width in widths],
        [(rows, width) for width in widths],
        layer,
        held,
    )


def row_outputs(gathered, layer, held, ff):
    rows = gathered.shape[1]
    by = lambda i: (0, i)
    heights = (XW, HD, ff)
    blocks = [((rows, PAR * ff), by)] * 2 + [((PAR * h, rows), by) for h in heights]
    shapes = [(rows, TP * ff)] * 2 + [(PAR * h, ZZ * rows) for h in heights]
    return assembled(
        rows_kernel,
        gathered,
        pl.BlockSpec((PAR, rows, gathered.shape[2]), lambda i: (i, 0, 0)),
        ZZ,
        blocks,
        shapes,
        layer,
        held,
    )


def layer_forward(h, w, meta):
    marks, seg_rows, seg_all, tables = meta
    inv1 = inv_rms(h)
    normed = (h * inv1 * w["norm_gain"]).astype(BF)
    p = dot(normed, w["w1"])
    ssd, gated, squares, states = ssd_forward(p, marks, seg_rows, w)
    square = tp_sum(squares)
    q, k, v, attended, logs = attn_forward(p, tables, marks, seg_all)
    inv_g = lax.rsqrt(square.reshape(-1) / DSSM + EPSILON)[:, None]
    mixer = (gated * inv_g * w["gain"]).astype(BF)
    mixed = jnp.concatenate([mixer, attended.astype(BF)], axis=1)
    mid = h + lax.psum(dot(mixed, w["wr"][: XW + HD]).astype(BF), TPA).astype(F32)
    inv2 = inv_rms(mid)
    normed2 = (mid * inv2 * w["ffn_gain"]).astype(BF)
    gu = dot(normed2, w["w2"])
    ff = gu.shape[1] // 2
    act = (jax.nn.silu(gu[:, :ff]) * gu[:, ff:]).astype(BF)
    kept = dict(
        h=h, inv1=inv1, normed=normed, p=p, ssd=ssd, gated=gated, states=states, inv_g=inv_g,
        q=q, k=k, v=v, attended=attended, logs=logs, mixed=mixed, mid=mid, inv2=inv2,
        normed2=normed2, gu=gu, act=act,
    )
    return mid, act, kept


def layer_backward(gout, w, kept, meta, reduce_rows, pending, finish):
    marks, seg_rows, seg_all, tables = meta
    g_down = gout.astype(BF)
    g_act = dot_nt(g_down, w["wr"][XW + HD :])
    d_down = dot_tn(g_down, kept["act"])
    ff = kept["gu"].shape[1] // 2
    gate, up = kept["gu"][:, :ff], kept["gu"][:, ff:]
    sig = jax.nn.sigmoid(gate)
    g_gate = g_act * up * sig * (1.0 + gate * (1.0 - sig))
    g_up = g_act * gate * sig
    g_gu = jnp.concatenate([g_gate.astype(BF), g_up.astype(BF)], axis=1)
    part_2 = dot_nt(g_gu, w["w2"]).astype(BF)
    g_n2 = lax.psum(part_2, TPA).astype(F32)
    d_ffn_gain = gain_back(part_2, kept["mid"], kept["inv2"])
    d_w2 = dot_tn(kept["normed2"], g_gu)
    g_mid = gout + rms_back(g_n2, kept["mid"], kept["inv2"], w["ffn_gain"])
    g_low = g_mid.astype(BF)
    g_mixed = dot_nt(g_low, w["wr"][: XW + HD])
    d_wr = dot_tn(g_low, kept["mixed"])
    early = reduce_rows(d_w2, d_wr, d_down)
    weighted = g_mixed[:, :XW] * w["gain"] * kept["gated"] * kept["inv_g"]
    mean = tp_sum(jnp.sum(weighted, axis=-1))[:, None] / DSSM
    scale = jnp.concatenate([kept["inv_g"], mean], axis=1)
    held, d_taps, d_small = ssd_backward(
        kept["p"], marks, seg_rows, kept["ssd"], g_mixed, scale, kept["states"], w
    )
    g_pr = attn_backward(
        held, kept["q"], kept["k"], kept["v"], kept["attended"], kept["logs"], g_mixed, tables,
        marks, seg_all,
    )
    g_pr, pending = lax.optimization_barrier((g_pr, pending))
    part_1 = dot_nt(g_pr, w["w1"]).astype(BF)
    if finish is None:
        g_n1 = lax.psum(part_1, TPA).astype(F32)
        g_h = g_mid + rms_back(g_n1, kept["h"], kept["inv1"], w["norm_gain"])
    else:
        g_h = finish(g_pr, g_mid)
    d_w1 = dot_tn(kept["normed"], g_pr)
    d_norm_gain = gain_back(part_1, kept["h"], kept["inv1"])
    d_skip = jnp.sum(d_small[1, :XW].reshape(HEADS, MP), axis=1)
    at = slice(DTL, DTL + HEADS)
    small = (
        d_norm_gain, d_taps[:CONV], d_taps[CONV], d_small[2, at], d_small[3, at], d_skip,
        d_small[0, :XW], d_ffn_gain,
    )
    return g_h, d_w1, early, pending, small


def per_device(
    block_in,
    seq_lengths,
    norm_gain,
    in_proj,
    conv_weight,
    conv_bias,
    dt_bias,
    decay_log,
    skip_gain,
    mixer_gain,
    out_proj,
    query_proj,
    key_proj,
    value_proj,
    attn_proj,
    ffn_gain,
    gate_proj,
    up_proj,
    down_proj,
    out_grad,
):
    fs = lax.axis_size("fsdp")
    reps = lax.axis_size("rep")
    ctx = reps * TP
    own_rows, width = block_in.shape
    rows = ctx * own_rows
    f = lax.axis_index("fsdp")
    rep = lax.axis_index("rep")
    t = lax.axis_index(TPA)
    every = ("rep",) + TPA

    lengths = seq_lengths[0]
    ends = jnp.cumsum(lengths)
    starts = ends - lengths
    line = jnp.arange(rows, dtype=jnp.int32)
    seg = jnp.sum((line[:, None] >= ends[None, :]).astype(jnp.int32), axis=1)
    pos = line - jnp.sum(jnp.where(seg[:, None] == jnp.arange(SEQS)[None, :], starts[None, :], 0), axis=1)
    pieces = lengths // ctx
    p_ends = jnp.cumsum(pieces)
    p_starts = p_ends - pieces

    def placed(piece):
        local = line[: piece.shape[0]] % own_rows
        l_seg = jnp.sum((local[:, None] >= p_ends[None, :]).astype(jnp.int32), axis=1)
        pick = l_seg[:, None] == jnp.arange(SEQS)[None, :]
        moved = starts[None, :] - p_starts[None, :] + piece[:, None] * pieces[None, :]
        return jnp.sum(jnp.where(pick, moved, 0), axis=1) + local

    slot = line // own_rows
    near = (lax.axis_index("zz") ^ (slot % ZZ)) * PAR
    near = near + (lax.axis_index("par") ^ (slot // ZZ % PAR))
    place_rel = placed(slot // TP * TP + near)
    half = HD // 2
    frequency = jnp.exp(-math.log(ROPE_BASE) * jnp.arange(half, dtype=F32) / half)
    angles = pos.astype(F32)[:, None] * frequency[None, :]
    cosine, sine = jnp.cos(angles), jnp.sin(angles)
    tables = (
        jnp.concatenate([cosine, cosine], axis=1),
        jnp.concatenate([-sine, sine], axis=1),
    )
    size = min(CHUNK, rows)
    by_chunk = seg.reshape(-1, size)
    last_seg = by_chunk[:, -1:]
    prev_seg = jnp.concatenate([jnp.full((1, 1), -1, last_seg.dtype), last_seg[:-1]], 0)
    ahead = jnp.concatenate([pos, jnp.zeros((CONV - 1,), pos.dtype)])
    marks = [seg, (by_chunk == prev_seg).reshape(-1), (by_chunk == last_seg).reshape(-1)]
    marks += [pos >= lag for lag in range(1, CONV)]
    marks += [ahead[lag : lag + rows] >= lag for lag in range(1, CONV)]
    marks = jnp.stack([m.astype(F32) for m in marks] + [jnp.zeros((rows,), F32)] * 7, axis=1)
    seg_f = seg.astype(F32)
    meta = (marks, seg_f.reshape(-1, 1, size), seg_f.reshape(1, rows), tables)

    to_seq = one_hot(place_rel, rows).T

    def cut(array, layer, at, count, axis):
        begin = [layer, 0, 0]
        extent = [1] + list(array.shape[1:])
        begin[axis], extent[axis] = at, count
        return lax.dynamic_slice(array, begin, extent)[0]

    ff = gate_proj.shape[2] // TP
    own_kv = HD * (t * KVH // TP)
    depth = in_proj.shape[1]

    def columns_1(layer):
        return jnp.concatenate(
            [
                in_proj[layer, :, 2 * DSSM : DSSM + CONVCH],
                cut(in_proj, layer, DSSM + XW * t, XW, 2),
                jnp.zeros((depth, 64), BF),
                cut(in_proj, layer, XW * t, XW, 2),
                cut(in_proj, layer, DSSM + CONVCH + HEADS * t, HEADS, 2),
                jnp.zeros((depth, 64 - HEADS), BF),
                cut(query_proj, layer, HD * t, HD, 2),
                cut(key_proj, layer, own_kv, HD, 2),
                cut(value_proj, layer, own_kv, HD, 2),
            ],
            1,
        )

    def columns_2(layer):
        return jnp.concatenate(
            [cut(gate_proj, layer, ff * t, ff, 2), cut(up_proj, layer, ff * t, ff, 2)], 1
        )

    par = t % PAR

    def row_chunk(layer):
        whole = jnp.concatenate(
            [
                cut(out_proj, layer, XW * par, XW, 1),
                cut(attn_proj, layer, HD * par, HD, 1),
                cut(down_proj, layer, ff * par, ff, 1),
            ],
            0,
        )
        part = whole.shape[0] // ZZ
        return lax.dynamic_slice_in_dim(whole, lax.axis_index("zz") * part, part, 0)

    forth = []
    for s in range(fs):
        for r in range(reps):
            for c in range(TP):
                src = (s * reps + r) * TP + c
                dst = ((c // PAR) * reps + r) * TP + PAR * s + c % PAR
                forth.append((src, dst))
    back = [(b, a) for a, b in forth]
    axes = ("fsdp",) + every

    smalls = jnp.concatenate(
        [
            norm_gain,
            conv_weight.transpose(0, 2, 1).reshape(LAYERS, -1),
            conv_bias,
            dt_bias,
            decay_log,
            skip_gain,
            mixer_gain,
            ffn_gain,
        ],
        axis=1,
    )
    w1 = [gathered_rows(columns_1(0), "fsdp"), None]
    x_all = group_tokens(block_in)
    small_all = gathered_rows(smalls[None], "fsdp")
    w2 = [None, None]
    wr = [None, None]
    x_all, w1[0], others, own_grad = lax.optimization_barrier(
        (
            x_all,
            w1[0],
            ([row_chunk(i) for i in range(LAYERS)], [columns_2(i) for i in range(LAYERS)], columns_1(1)),
            out_grad,
        )
    )
    wr[0] = gathered_rows(lax.ppermute(others[0][0], axes, forth), "fsdp")
    w2[0] = gathered_rows(others[1][0], "fsdp")
    w1[1] = gathered_rows(others[2], "fsdp")
    wr[1] = gathered_rows(lax.ppermute(others[0][1], axes, forth), "fsdp")
    w2[1] = gathered_rows(others[1][1], "fsdp")
    g_all = group_tokens(own_grad)

    sizes = [
        norm_gain.shape[1],
        CONV * conv_weight.shape[1],
        conv_bias.shape[1],
        dt_bias.shape[1],
        decay_log.shape[1],
        skip_gain.shape[1],
        mixer_gain.shape[1],
        ffn_gain.shape[1],
    ]
    offsets = [sum(sizes[:i]) for i in range(len(sizes) + 1)]

    def own_conv(full):
        return jnp.concatenate(
            [full[..., DSSM:], lax.dynamic_slice_in_dim(full, XW * t, XW, full.ndim - 1)], -1
        )

    weights = []
    for layer in range(LAYERS):
        part = [
            small_all[:, layer, offsets[i] : offsets[i + 1]].astype(F32) for i in range(len(sizes))
        ]
        cw = part[1].reshape(fs, CONV, -1).transpose(1, 0, 2).reshape(CONV, CONVCH)
        full = [p.reshape(-1) for p in part]
        weights.append(
            dict(
                w1=w1[layer],
                w2=w2[layer],
                wr=wr[layer],
                norm_gain=full[0],
                taps=jnp.concatenate(
                    [own_conv(cw), own_conv(full[2])[None], jnp.zeros((3, CW), F32)], 0
                ),
                heads=jnp.zeros((8, 128), F32)
                .at[0, DTL : DTL + HEADS]
                .set(lax.dynamic_slice_in_dim(full[3], HEADS * t, HEADS, 0))
                .at[1, DTL : DTL + HEADS]
                .set(jnp.exp(lax.dynamic_slice_in_dim(full[4], HEADS * t, HEADS, 0))),
                skip=jnp.repeat(lax.dynamic_slice_in_dim(full[5], HEADS * t, HEADS, 0), MP)[None],
                gain=lax.dynamic_slice_in_dim(full[6], XW * t, XW, 0)[None],
                ffn_gain=full[7],
            )
        )

    h = dot(to_seq, x_all)
    saved = []
    for layer in range(LAYERS):
        mid, act, kept = layer_forward(h, weights[layer], meta)
        saved.append(kept)
        if layer < LAYERS - 1:
            h = mid + lax.psum(dot(act, weights[layer]["wr"][XW + HD :]).astype(BF), TPA).astype(F32)

    own_hot = one_hot(placed(jnp.full((own_rows,), rep * TP + t, jnp.int32)), rows)
    rep_place = placed(rep * TP + line[: TP * own_rows] // own_rows)
    rep_hot = one_hot(rep_place, rows)
    act_rep = dot(rep_hot, act).astype(BF)
    down_own = lax.psum_scatter(
        dot(act_rep, weights[-1]["wr"][XW + HD :]).astype(BF), TPA, scatter_dimension=0, tiled=True
    )
    mid_own = jnp.dot(
        own_hot.astype(F32), mid, precision=lax.Precision.HIGHEST, preferred_element_type=F32
    )

    gout = dot(to_seq, g_all)

    def reduce_rows(d_w2, d_wr, d_down):
        d_all = jnp.concatenate([d_w2.astype(BF), d_wr.astype(BF), d_down.astype(BF)], 1)
        part = scattered_rows(d_all, "fsdp").astype(BF)
        kept_cols = d_w2.shape[1]
        moved = lax.ppermute(part[:, kept_cols:], axes, back)
        held = jnp.zeros((part.shape[0], 64), BF)
        part = jnp.concatenate([part[:, :kept_cols], moved, held], 1)
        return part

    def reduce_columns(d_w1, small_grads):
        g_n, g_cw, g_cb, g_db, g_dl, g_sk, g_mg, g_fg = small_grads
        small = jnp.concatenate(
            [g_n, g_cw.reshape(-1), g_cb, g_db, g_dl, g_sk, g_mg, g_fg]
        )
        others = [swapped(small, "fsdp", by) for by in range(1, fs)]
        for other in others:
            small = small + other
        part = scattered_rows(d_w1.astype(BF), "fsdp").astype(BF)
        held = jnp.zeros((part.shape[0] * 64,), BF)
        high = small.astype(BF)
        low = (small - lax.optimization_barrier(high).astype(F32)).astype(BF)
        held = lax.dynamic_update_slice(held, jnp.concatenate([high, low]), (0,)).reshape(-1, 64)
        return jnp.concatenate([part[:, :CW], held, part[:, 512:]], 1)

    def finish(g_pr, g_mid):
        moved = dot(rep_hot, g_pr).astype(BF)
        own = lax.psum_scatter(
            dot_nt(moved, weights[0]["w1"]).astype(BF), TPA, scatter_dimension=0, tiled=True
        ).astype(F32)
        mid = jnp.dot(
            own_hot.astype(F32), g_mid, precision=lax.Precision.HIGHEST, preferred_element_type=F32
        )
        h_own = block_in.astype(F32)
        return mid + rms_back(own, h_own, inv_rms(h_own), weights[0]["norm_gain"])

    gout, d_w1, early, down_own, small_grads = layer_backward(
        gout, weights[1], saved[1], meta, reduce_rows, down_own, None
    )
    block_out = (mid_own + down_own.astype(F32)).astype(BF)
    late = reduce_columns(d_w1, small_grads)
    pending = (lax.all_gather(early, TPA, axis=0), late)
    in_grad, d_w1, early, pending, small_grads = layer_backward(
        gout, weights[0], saved[0], meta, reduce_rows, pending, finish
    )
    in_grad = in_grad.astype(BF)
    rows_1, late = pending
    both = lax.all_gather(jnp.concatenate([late, early], 1), TPA, axis=0)
    split = late.shape[1]
    columns_0 = lax.all_gather(reduce_columns(d_w1, small_grads), TPA, axis=0)
    columns_of = [columns_0, both[:, :, :split]]
    held = row_outputs(rows_1, 1, None, ff)
    o_gate, o_up, o_out, o_attn, o_down = row_outputs(both[:, :, split:], 0, held, ff)
    held = column_outputs(columns_of[1], 1, None)
    o_in, o_q, o_k, o_v = column_outputs(columns_of[0], 0, held)

    own_sizes = [width, CONV * CW, CW, HEADS, HEADS, HEADS, XW, width]
    own_at = [sum(own_sizes[:i]) for i in range(len(own_sizes) + 1)]
    outs_small = [[] for _ in sizes]

    def conv_full(parts):
        parts = parts.astype(F32)
        return jnp.concatenate(
            [
                jnp.moveaxis(parts[..., 2 * NS :], 0, -2).reshape(parts.shape[1:-1] + (DSSM,)),
                jnp.sum(parts[..., : 2 * NS], axis=0),
            ],
            -1,
        )

    for layer in range(LAYERS):
        held = columns_of[layer][:, :, CW:512].astype(F32).reshape(TP, -1)
        held = held[:, : own_at[-1]] + held[:, own_at[-1] : 2 * own_at[-1]]
        parts = [held[:, own_at[i] : own_at[i + 1]] for i in range(len(own_sizes))]
        full = [
            jnp.sum(parts[0].astype(F32), axis=0),
            conv_full(parts[1].reshape(TP, CONV, CW)).T.reshape(-1),
            conv_full(parts[2]),
        ]
        full += [p.astype(F32).reshape(-1) for p in parts[3:7]] + [jnp.sum(parts[7].astype(F32), axis=0)]
        for i, vec in enumerate(full):
            own = vec.shape[0] // fs
            outs_small[i].append(lax.dynamic_slice_in_dim(vec, own * f, own, 0))
    (o_norm, o_cw, o_cb, o_db, o_dl, o_sk, o_mg, o_fg) = [jnp.stack(o) for o in outs_small]
    o_cw = o_cw.reshape(LAYERS, -1, CONV)

    return (
        block_out,
        in_grad,
        o_norm,
        o_in,
        o_cw,
        o_cb,
        o_db,
        o_dl,
        o_sk,
        o_mg,
        o_out,
        o_q,
        o_k,
        o_v,
        o_attn,
        o_fg,
        o_gate,
        o_up,
        o_down,
    )


def solution(mesh):
    fs = mesh.shape["fsdp"]
    inner = Mesh(
        mesh.devices.reshape(fs, mesh.shape["ctx"] // TP, ZZ, PAR), ("fsdp", "rep", "zz", "par")
    )
    tokens = P(("fsdp", "rep", "zz", "par"), None)
    vec = P(None, "fsdp")
    mat = P(None, "fsdp", None)
    kinds = (
        vec, mat, mat, vec, vec, vec, vec, vec, mat, mat, mat, mat, mat, vec, mat, mat, mat
    )
    return jax.shard_map(
        per_device,
        mesh=inner,
        in_specs=(tokens, P("fsdp", None)) + kinds + (tokens,),
        out_specs=(tokens, tokens) + kinds,
        check_vma=False,
    )
```
